512 devices in a mesh: ctx: 128 (over y, z, core), tp: 4 (over x).
Axes of the slice: x: 4, y: 4, z: 16, core: 2. Of those that a mesh axis runs over, the one named last changes fastest.
Arguments:
- query_raw: bfloat16 [1, 32768, 4096], P(None, 'ctx', 'tp'), may hold values from -6 to 6
- key_raw: bfloat16 [1, 32768, 4096], P(None, 'ctx', 'tp'), may hold values from -6 to 6
- value_raw: bfloat16 [1, 32768, 4096], P(None, 'ctx', 'tp'), may hold values from -6 to 6
- cotangent: bfloat16 [1, 32768, 4096], P(None, 'ctx', 'tp'), may hold values from -40 to 40
- featurizer: float32 [3, 7, 4096], P(None, None, 'tp'), may hold values from -1.6 to 1.6
- filters: bfloat16 [256, 128], P('tp'), may hold values from -0.5 to 0.5
Outputs:
- grad_query: bfloat16 [1, 32768, 4096], P(None, 'ctx', 'tp')
- grad_key: bfloat16 [1, 32768, 4096], P(None, 'ctx', 'tp')
- grad_value: bfloat16 [1, 32768, 4096], P(None, 'ctx', 'tp')
- grad_featurizer: float32 [3, 7, 4096], P(None, None, 'tp')
- grad_filters: float32 [256, 128], P('tp')
The draws below stay inside these ranges and needn't reach their ends.
All inputs are finite; a program needn't handle non-finite values.
Results may differ from the reference program's by a relative error of at most 0.0055.
Values may be sent and summed in bfloat16 or wider, within the bound.
A program may use at most 128 MiB of HBM per device.

```python
import math
import jax
import jax.numpy as jnp
from jax import lax

SEQS = 1
CHANNELS = 4096
GROUP_SIZE = 16
FEAT_TAPS = 7
FILTER_TAPS = 128
LENGTH = 32768
GROUPS = 256


def draw_cotangent(key, part):
    key = jax.random.fold_in(key, 23)
    positions = jnp.arange(LENGTH, dtype=jnp.float32)[None, :, None] / max(LENGTH - 1, 1)
    channel_pos = jnp.arange(CHANNELS, dtype=jnp.float32)[None, None, :] / max(CHANNELS - 1, 1)
    envelope = jnp.exp(jnp.log(3.0) * (positions + channel_pos))
    base = jnp.clip(jax.random.normal(key, (SEQS, LENGTH, CHANNELS), jnp.float32), -4.0, 4.0)
    return (base * envelope).astype(jnp.bfloat16)


def draw_filters(key, part):
    key = jax.random.fold_in(key, 11)
    key_decay, key_shape = jax.random.split(key)
    decay_rate = jnp.exp(jax.random.uniform(key_decay, (GROUPS, 1), jnp.float32, jnp.log(1.0 / 3000.0), jnp.log(1.0 / 30.0)))
    lag_index = jnp.arange(FILTER_TAPS, dtype=jnp.float32)[None, :]
    roughness = jnp.clip(jax.random.normal(key_shape, (GROUPS, FILTER_TAPS), jnp.float32), -4.0, 4.0)
    return (0.12 * roughness * jnp.exp(-decay_rate * lag_index)).astype(jnp.bfloat16)


def levels(stream_key, dims, shards, low, top_value):
    def one(dim, parts):
        steps = jax.random.uniform(jax.random.fold_in(jax.random.fold_in(stream_key, 6), dim), (parts,), jnp.float32, low / len(shards), top_value / len(shards))
        return jnp.repeat(jnp.exp(steps), dims[dim] // parts).reshape((-1,) + (1,) * (len(dims) - dim - 1))

    level = one(*shards[0])
    for cut in shards[1:]:
        level = level * one(*cut)
    return level


def noise(stream_key, dims, scale, limit, cuts=(), kind=jnp.bfloat16):
    drawn = scale * jax.random.normal(stream_key, dims, jnp.float32)
    if cuts:
        drawn = drawn * levels(stream_key, dims, cuts, -0.22, 0.18)
    return jnp.clip(drawn, -limit, limit).astype(kind)


def setup_inputs(seed: int = 0) -> dict:
    key_list = jax.random.split(jax.random.key(seed), 7)
    query_raw = noise(key_list[0], (SEQS, LENGTH, CHANNELS), 1.0, 6.0, ((1, 128), (2, 4)))
    key_raw = noise(key_list[1], (SEQS, LENGTH, CHANNELS), 1.0, 6.0, ((1, 128), (2, 4)))
    value_raw = noise(key_list[2], (SEQS, LENGTH, CHANNELS), 1.0, 6.0, ((1, 128), (2, 4)))
    cotangent = draw_cotangent(jax.random.fold_in(key_list[6], 71), 0)
    featurizer = noise(key_list[4], (3, FEAT_TAPS, CHANNELS), 0.4, 1.6, ((2, 4),), jnp.float32)
    filters = draw_filters(jax.random.fold_in(key_list[6], 71), 0)
    return {"query_raw": query_raw, "key_raw": key_raw, "value_raw": value_raw, "cotangent": cotangent, "featurizer": featurizer, "filters": filters}


clip_norm = 100.0

def band_table(filters, lagged):
    inside = (lagged >= 0) & (lagged < FILTER_TAPS)
    picked = jnp.take(filters, jnp.clip(lagged, 0, FILTER_TAPS - 1), axis=1)
    return jnp.where(inside[None], picked, jnp.zeros_like(picked))

def causal_table(filters):
    lag_rows = jnp.arange(FILTER_TAPS)[:, None]
    lag_cols = jnp.arange(2 * FILTER_TAPS)[None, :]
    return band_table(filters, lag_rows + FILTER_TAPS - lag_cols)

def reverse_table(filters):
    lag_rows = jnp.arange(FILTER_TAPS)[:, None]
    lag_cols = jnp.arange(2 * FILTER_TAPS)[None, :]
    return band_table(filters, lag_cols - lag_rows)

def featurize(extended, weight, row_count):
    offset = extended.shape[-2] - row_count - (FEAT_TAPS - 1)
    summed = jnp.zeros(extended.shape[:-2] + (row_count, extended.shape[-1]), jnp.float32)
    for tap_index in range(FEAT_TAPS):
        first = offset + FEAT_TAPS - 1 - tap_index
        summed = summed + weight[tap_index] * extended[..., first:first + row_count, :].astype(jnp.float32)
    return summed

def adjoint(delta_ext, weight, row_count):
    summed = jnp.zeros(delta_ext.shape[:-2] + (row_count, delta_ext.shape[-1]), jnp.float32)
    for tap_index in range(FEAT_TAPS):
        summed = summed + weight[tap_index] * delta_ext[..., tap_index:tap_index + row_count, :]
    return summed

def tap_grads(delta, extended, row_count):
    offset = extended.shape[-2] - row_count - (FEAT_TAPS - 1)
    collected = []
    for tap_index in range(FEAT_TAPS):
        first = offset + FEAT_TAPS - 1 - tap_index
        piece = extended[..., first:first + row_count, :].astype(jnp.float32)
        collected.append(lax.optimization_barrier(jnp.sum(delta * piece, axis=(0, 1))))
    return jnp.stack(collected, axis=0)

def skew_sum(moment):
    groups = moment.shape[0]
    flattened = moment.reshape(groups, 2 * FILTER_TAPS * FILTER_TAPS)
    flattened = jnp.pad(flattened, ((0, 0), (0, FILTER_TAPS)))
    skewed = flattened[:, :FILTER_TAPS * (2 * FILTER_TAPS + 1)].reshape(groups, FILTER_TAPS, 2 * FILTER_TAPS + 1)
    return lax.optimization_barrier(jnp.sum(skewed[:, :, 1:FILTER_TAPS + 1], axis=1))[:, ::-1]

def span(query_raw, key_raw, value_raw, cotangent, weight, filters):
    seq_len = query_raw.shape[1]
    channel_count = query_raw.shape[2]
    groups = filters.shape[0]
    tile_count = seq_len // FILTER_TAPS
    front = ((0, 0), (FEAT_TAPS - 1, 0), (0, 0))
    query_ext = jnp.pad(query_raw, front)
    key_ext = jnp.pad(key_raw, front)
    value_ext = jnp.pad(value_raw, front)
    query_feat = featurize(query_ext, weight[0], seq_len)
    key_feat = featurize(key_ext, weight[1], seq_len)
    value_feat = featurize(value_ext, weight[2], seq_len)
    product = (key_feat * value_feat).astype(jnp.bfloat16)
    product_ext = jnp.pad(product, ((0, 0), (FILTER_TAPS, 0), (0, 0)))
    tile_shape = (1, tile_count, FILTER_TAPS, groups, GROUP_SIZE)
    earlier = product_ext[:, :seq_len].reshape(tile_shape).astype(jnp.float32)
    current = product_ext[:, FILTER_TAPS:].reshape(tile_shape).astype(jnp.float32)
    forward_table = causal_table(filters).astype(jnp.float32)
    convolved = jnp.einsum('gts,bnsgc->bntgc', forward_table[:, :, :FILTER_TAPS], earlier)
    convolved = convolved + jnp.einsum('gts,bnsgc->bntgc', forward_table[:, :, FILTER_TAPS:], current)
    convolved = convolved.reshape(1, seq_len, channel_count)
    upstream = cotangent.astype(jnp.float32)
    mid_grad = (upstream * query_feat).astype(jnp.bfloat16)
    query_delta = upstream * convolved
    mid_ext = jnp.pad(mid_grad, ((0, 0), (0, FILTER_TAPS), (0, 0)))
    mid_tiles = mid_grad.reshape(tile_shape).astype(jnp.float32)
    following = mid_ext[:, FILTER_TAPS:].reshape(tile_shape).astype(jnp.float32)
    backward_table = reverse_table(filters).astype(jnp.float32)
    product_grad = jnp.einsum('gst,bntgc->bnsgc', backward_table[:, :, :FILTER_TAPS], mid_tiles)
    product_grad = product_grad + jnp.einsum('gst,bntgc->bnsgc', backward_table[:, :, FILTER_TAPS:], following)
    product_grad = product_grad.reshape(1, seq_len, channel_count)
    key_delta = product_grad * value_feat
    value_delta = product_grad * key_feat
    tail = ((0, 0), (0, FEAT_TAPS - 1), (0, 0))
    grad_query = adjoint(jnp.pad(query_delta, tail), weight[0], seq_len).astype(jnp.bfloat16)
    grad_key = adjoint(jnp.pad(key_delta, tail), weight[1], seq_len).astype(jnp.bfloat16)
    grad_value = adjoint(jnp.pad(value_delta, tail), weight[2], seq_len).astype(jnp.bfloat16)
    feat_grad = jnp.stack([tap_grads(query_delta, query_ext, seq_len), tap_grads(key_delta, key_ext, seq_len), tap_grads(value_delta, value_ext, seq_len)], axis=0)
    moment = jnp.concatenate([jnp.einsum('bntgc,bnsgc->gts', mid_tiles, earlier), jnp.einsum('bntgc,bnsgc->gts', mid_tiles, current)], axis=2)
    filter_grad = skew_sum(moment)
    return (grad_query[0], grad_key[0], grad_value[0], feat_grad, filter_grad)

def reference(query_raw, key_raw, value_raw, cotangent, featurizer, filters):
    channel_block = math.gcd(CHANNELS, 256)
    outs_query = []
    outs_key = []
    outs_value = []
    feat_total = jnp.zeros((3, FEAT_TAPS, CHANNELS), jnp.float32)
    filter_total = jnp.zeros((GROUPS, FILTER_TAPS), jnp.float32)
    for seq_index in range(SEQS):
        parts_query = []
        parts_key = []
        parts_value = []
        feat_parts = []
        filter_parts = []
        for offset in range(0, CHANNELS, channel_block):
            section = slice(offset, offset + channel_block)
            group_slice = slice(offset // GROUP_SIZE, (offset + channel_block) // GROUP_SIZE)
            result = span(query_raw[seq_index:seq_index + 1, :, section], key_raw[seq_index:seq_index + 1, :, section], value_raw[seq_index:seq_index + 1, :, section], cotangent[seq_index:seq_index + 1, :, section], featurizer[:, :, section], filters[group_slice])
            parts_query.append(result[0])
            parts_key.append(result[1])
            parts_value.append(result[2])
            feat_parts.append(result[3])
            filter_parts.append(result[4])
        outs_query.append(jnp.concatenate(parts_query, axis=1))
        outs_key.append(jnp.concatenate(parts_key, axis=1))
        outs_value.append(jnp.concatenate(parts_value, axis=1))
        feat_total = feat_total + jnp.concatenate(feat_parts, axis=2)
        filter_total = filter_total + jnp.concatenate(filter_parts, axis=0)
    squared = jnp.sum(feat_total * feat_total) + jnp.sum(filter_total * filter_total)
    factor = 1.0 / jnp.maximum(1.0, jnp.sqrt(squared) / clip_norm)
    return (jnp.stack(outs_query, axis=0), jnp.stack(outs_key, axis=0), jnp.stack(outs_value, axis=0), factor * feat_total, factor * filter_total)
```

```python
import jax
import jax.numpy as jnp
from jax import lax
from jax.experimental import pallas as pl
from jax.experimental.pallas import tpu as pltpu
from jax.sharding import PartitionSpec as P

GROUP = 16
TAPS = 7
LAGS = 128
LANES = 128
HALO = 16
BLOCK = 16
WIN = LAGS + BLOCK
CLIP = 100.0
F32 = jnp.float32
BF16 = jnp.bfloat16
MESH = pl.DeviceIdType.MESH
NY, NZ, NX = 4, 16, 4


def remote(src, dst, send, recv, device):
    return pltpu.make_async_remote_copy(
        src_ref=src, dst_ref=dst, send_sem=send, recv_sem=recv, device_id=device, device_id_type=MESH
    )


def kernel(
    q_ref,
    k_ref,
    v_ref,
    cot_ref,
    feat_ref,
    filt_ref,
    gq_ref,
    gk_ref,
    gv_ref,
    gfeat_ref,
    gfilt_ref,
    halo,
    raw,
    kfeat,
    vfeat,
    prod,
    mid,
    delta,
    tabs,
    fwd_tab,
    rev_tab,
    moment,
    pay,
    got1,
    got2,
    part,
    got3,
    full3,
    full,
    norms,
    norm2,
    s_halo,
    r_halo,
    s_big,
    r_big,
    s_del,
    r_del,
    s_core,
    r_core,
    s_y,
    r_y,
    s_z,
    r_z,
    s_xy,
    r_xy,
):
    rows, channels = q_ref.shape
    cols = channels // LANES
    per_col = LANES // GROUP
    groups = filt_ref.shape[0]
    half = rows // 2
    ctx = lax.axis_index("ctx")
    tp = lax.axis_index("tp")
    n_ctx = 2 * NY * NZ
    core = lax.rem(ctx, 2)
    zi = lax.rem(lax.div(ctx, 2), NZ)
    yi = lax.div(ctx, 2 * NZ)

    def at(x, y, z, c):
        return ((y * NZ + z) * 2 + c, x)

    first = ctx == 0
    last = ctx == n_ctx - 1
    after = (lax.rem(ctx + 1, n_ctx), tp)
    before = (lax.rem(ctx + n_ctx - 1, n_ctx), tp)
    twin = at(tp, yi, zi, 1 - core)
    z_peers = [at(tp, yi, lax.rem(zi + d, NZ), core) for d in range(1, NZ)]
    y_peers = [at(tp, lax.rem(yi + d, NY), zi, core) for d in range(1, NY)]
    xy_peers = [
        at(lax.rem(tp + dx, NX), lax.rem(yi + dy, NY), zi, core)
        for dx in range(NX)
        for dy in range(NY)
        if dx or dy
    ]

    barrier = pltpu.get_barrier_semaphore()
    greeted = [after, before] + z_peers + xy_peers
    for peer in greeted:
        pl.semaphore_signal(barrier, inc=1, device_id=peer, device_id_type=MESH)

    moment[2, pl.ds(0, 8), :] = jnp.zeros((8, LANES), F32)

    lag_row = lax.broadcasted_iota(jnp.int32, (LAGS, 2 * LANES), 0)
    lag_col = lax.broadcasted_iota(jnp.int32, (LAGS, 2 * LANES), 1)
    flip = jnp.where(lag_row + lag_col == LAGS, 1.0, 0.0).astype(BF16)
    keep = jnp.where(lag_row == lag_col, 1.0, 0.0).astype(BF16)
    for pick, table in ((flip, fwd_tab), (keep, rev_tab)):
        wide = jnp.dot(filt_ref[...], pick, preferred_element_type=F32)
        for b in range(BLOCK):
            moved = pltpu.roll(wide, b, 1) if b else wide
            tabs[0, pl.ds(b, groups, stride=BLOCK), :] = moved[:, :LANES]
            tabs[1, pl.ds(b, groups, stride=BLOCK), :] = moved[:, LANES:]
        for j in range(cols):
            span = pl.ds(j * LANES, LANES)
            table[j] = jnp.concatenate([tabs[0, span, :], tabs[1, span, :]], axis=1).astype(BF16)

    pl.semaphore_wait(barrier, len(greeted))

    halo_copies = [
        remote(ref.at[pl.ds(rows - HALO, HALO), :], halo.at[s], s_halo.at[s], r_halo.at[s], after)
        for s, ref in enumerate((q_ref, k_ref, v_ref))
    ]
    for copy in halo_copies:
        copy.start()

    def lanes_of(j):
        return pl.ds(pl.multiple_of(j * LANES, LANES), LANES)

    def weights(s, j):
        return [feat_ref[s, pl.ds(tap, 1), lanes_of(j)] for tap in range(TAPS)]

    def featurized(s, j, taps, start, count):
        total = taps[0] * raw[s, j, pl.ds(HALO + start, count), :]
        for tap in range(1, TAPS):
            total = total + taps[tap] * raw[s, j, pl.ds(HALO + start - tap, count), :]
        return total

    chunk = 64

    def products(j, starts):
        k_taps, v_taps = weights(1, j), weights(2, j)
        for start in starts:
            here = pl.ds(start, chunk)
            k_here = featurized(1, j, k_taps, start, chunk)
            v_here = featurized(2, j, v_taps, start, chunk)
            kfeat[j, here, :] = k_here
            vfeat[j, here, :] = v_here
            prod[j, pl.ds(LAGS + start, chunk), :] = (k_here * v_here).astype(BF16)

    def mids(j, starts):
        q_taps = weights(0, j)
        for start in starts:
            here = pl.ds(start, chunk)
            q_here = featurized(0, j, q_taps, start, chunk)
            upstream = cot_ref[here, lanes_of(j)].astype(F32)
            mid[j, here, :] = (upstream * q_here).astype(BF16)

    @pl.loop(0, cols)
    def _(j):
        for s, ref in enumerate((q_ref, k_ref, v_ref)):
            raw[s, j, pl.ds(HALO, rows), :] = ref[:, lanes_of(j)].astype(F32)
        products(j, range(half, rows, chunk))

    send_prod = remote(
        prod.at[:, pl.ds(rows, LAGS), :], prod.at[:, pl.ds(0, LAGS), :], s_big.at[0], r_big.at[0], after
    )
    send_prod.start()

    for copy in halo_copies:
        copy.wait_recv()

    @pl.loop(0, cols)
    def _(j):
        for s in range(3):
            got = halo[s, :, lanes_of(j)].astype(F32)
            raw[s, j, pl.ds(0, HALO), :] = jnp.where(first, 0.0, got)
        mids(j, range(0, half, chunk))

    send_mid = remote(
        mid.at[:, pl.ds(0, LAGS), :], mid.at[:, pl.ds(rows, LAGS), :], s_big.at[1], r_big.at[1], before
    )
    send_mid.start()

    @pl.loop(0, cols)
    def _(j):
        mids(j, range(half, rows, chunk))
        products(j, range(0, half, chunk))

    lane_group = lax.broadcasted_iota(jnp.int32, (BLOCK, LANES), 1) // GROUP

    def picked(stacked, lane0):
        out = stacked[0:BLOCK, lane0 : lane0 + LANES]
        for g in range(1, per_col):
            piece = stacked[g * BLOCK : (g + 1) * BLOCK, lane0 : lane0 + LANES]
            out = jnp.where(lane_group == g, piece, out)
        return out

    def window(ref, j, a):
        near = ref[j, pl.ds(a * BLOCK, WIN), :]
        far = ref[j, pl.ds(a * BLOCK + half, WIN), :]
        return jnp.concatenate([near, far], axis=1)

    def tap_sums(j, s, acc, d, start, count):
        out = []
        for tap in range(TAPS):
            moved = raw[s, j, pl.ds(HALO + start - tap, count), :]
            term = jnp.sum((d * moved).reshape(count // 8, 8, LANES), axis=0)
            out.append(term if acc is None else acc[tap] + term)
        return out

    send_prod.wait_recv()

    @pl.when(first)
    def _():
        prod[:, pl.ds(0, LAGS), :] = jnp.zeros((cols, LAGS, LANES), BF16)

    @pl.loop(0, cols)
    def _(j):
        band = fwd_tab[j][:, :WIN]
        acc = None
        for a in range(half // BLOCK):
            stacked = jnp.dot(band, window(prod, j, a), preferred_element_type=F32)
            for side in range(2):
                start = a * BLOCK + side * half
                upstream = cot_ref[pl.ds(start, BLOCK), lanes_of(j)].astype(F32)
                d = upstream * picked(stacked, side * LANES)
                delta[0, j, pl.ds(start, BLOCK), :] = d
                acc = tap_sums(j, 0, acc, d, start, BLOCK)
        for tap in range(TAPS):
            moment[2, pl.ds(tap, 1), :] = jnp.sum(acc[tap], axis=0, keepdims=True)
        pay[j, pl.ds(0, 8), :] = moment[2, pl.ds(0, 8), :]

    send_mid.wait_recv()

    @pl.when(last)
    def _():
        mid[:, pl.ds(rows, LAGS), :] = jnp.zeros((cols, LAGS, LANES), BF16)

    row_group = lax.broadcasted_iota(jnp.int32, (LANES, 2 * LANES), 0) // BLOCK
    col_group = lax.rem(lax.broadcasted_iota(jnp.int32, (LANES, 2 * LANES), 1), LANES) // GROUP
    own = jnp.where(row_group == col_group, 1.0, 0.0).astype(BF16)

    @pl.loop(0, cols)
    def _(j):
        band = rev_tab[j][:, :WIN]
        acc_k = None
        acc_v = None
        pairs = jnp.zeros((LANES, WIN), F32)
        for a in range(half // BLOCK):
            ahead = window(mid, j, a)
            stacked = jnp.dot(band, ahead, preferred_element_type=F32)
            for side in range(2):
                start = a * BLOCK + side * half
                here = pl.ds(start, BLOCK)
                pg = picked(stacked, side * LANES)
                dk = pg * vfeat[j, here, :]
                dv = pg * kfeat[j, here, :]
                delta[1, j, here, :] = dk
                delta[2, j, here, :] = dv
                acc_k = tap_sums(j, 1, acc_k, dk, start, BLOCK)
                acc_v = tap_sums(j, 2, acc_v, dv, start, BLOCK)
            base = jnp.concatenate(
                [
                    prod[j, pl.ds(LAGS + a * BLOCK, BLOCK), :],
                    prod[j, pl.ds(LAGS + a * BLOCK + half, BLOCK), :],
                ],
                axis=1,
            )
            spread = jnp.concatenate([base] * per_col, axis=0) * own
            pairs = pairs + lax.dot_general(
                spread, ahead, (((1,), (1,)), ((), ())), preferred_element_type=F32
            )
        for s, acc in ((1, acc_k), (2, acc_v)):
            for tap in range(TAPS):
                moment[2, pl.ds(tap, 1), :] = jnp.sum(acc[tap], axis=0, keepdims=True)
            pay[j, pl.ds(s * 8, 8), :] = moment[2, pl.ds(0, 8), :]
        moment[0] = pairs[:, :LANES]
        moment[1, :, pl.ds(0, BLOCK)] = pairs[:, LANES:]
        lags = moment[0, pl.ds(0, per_col, stride=BLOCK), :]
        for b in range(1, BLOCK):
            low = moment[0, pl.ds(b, per_col, stride=BLOCK), :]
            high = moment[1, pl.ds(b, per_col, stride=BLOCK), :]
            both = pltpu.roll(jnp.concatenate([low, high], axis=1), 2 * LANES - b, 1)
            lags = lags + both[:, :LANES]
        pay[j, pl.ds(24, per_col), :] = lags

    send_del = remote(
        delta.at[:, :, pl.ds(0, 8), :], delta.at[:, :, pl.ds(rows, 8), :], s_del.at[0], r_del.at[0], before
    )
    send_del.start()

    pieces = 2 * NY
    per_core = cols // 2
    core1 = remote(
        pay.at[pl.ds((1 - core) * per_core, per_core)], got1, s_core.at[0], r_core.at[0], twin
    )
    core1.start()

    def adjoint(s, out_ref):
        @pl.loop(0, cols)
        def _(j):
            taps = weights(s, j)
            for start in range(0, rows, chunk):
                total = taps[0] * delta[s, j, pl.ds(start, chunk), :]
                for tap in range(1, TAPS):
                    total = total + taps[tap] * delta[s, j, pl.ds(start + tap, chunk), :]
                out_ref[pl.ds(start, chunk), lanes_of(j)] = total.astype(BF16)

    send_del.wait_recv()

    @pl.when(last)
    def _():
        delta[:, :, pl.ds(rows, 8), :] = jnp.zeros((3, cols, 8, LANES), F32)

    adjoint(0, gq_ref)

    core1.wait_recv()
    got1[...] = got1[...] + pay[pl.ds(core * per_core, per_core)]
    y_rs = [
        remote(got1.at[lax.rem(yi + d, NY)], got2.at[d - 1], s_y.at[d - 1], r_y.at[d - 1], y_peers[d - 1])
        for d in range(1, NY)
    ]
    for copy in y_rs:
        copy.start()

    adjoint(1, gk_ref)

    for copy in y_rs:
        copy.wait_recv()
    mine = got1[yi]
    for d in range(NY - 1):
        mine = mine + got2[d]
    for r in range(2 * NZ):
        part[r // 2, pl.ds(r % 2, 1), :] = mine[r : r + 1, :]
    z_rs = [
        remote(part.at[lax.rem(zi + d, NZ)], got3.at[d - 1], s_z.at[d - 1], r_z.at[d - 1], z_peers[d - 1])
        for d in range(1, NZ)
    ]
    for copy in z_rs:
        copy.start()

    adjoint(2, gv_ref)

    for copy in z_rs:
        copy.wait_recv()
    piece = part[zi]
    for d in range(NZ - 1):
        piece = piece + got3[d]
    full3[zi] = piece

    z_ag = [
        remote(full3.at[zi], full3.at[zi], s_z.at[NZ - 1 + d - 1], r_z.at[NZ - 1 + d - 1], z_peers[d - 1])
        for d in range(1, NZ)
    ]
    for copy in z_ag:
        copy.start()
    for d in range(1, NZ):
        src = lax.rem(zi + NZ - d, NZ)
        remote(
            full3.at[src], full3.at[src], s_z.at[NZ - 1 + d - 1], r_z.at[NZ - 1 + d - 1], z_peers[d - 1]
        ).wait_recv()
    slot = core * NY + yi
    for r in range(2 * NZ):
        full[slot, pl.ds(r, 1), :] = full3[r // 2, pl.ds(r % 2, 1), :]
    whole = full[slot]
    squares = jnp.sum(jnp.sum(whole * whole, axis=0, keepdims=True), axis=1, keepdims=True)
    norms[tp * NY + yi] = jnp.broadcast_to(squares, (8, LANES))
    y_ag = [
        remote(full.at[slot], full.at[slot], s_y.at[NY - 1 + d - 1], r_y.at[NY - 1 + d - 1], y_peers[d - 1])
        for d in range(1, NY)
    ]
    for copy in y_ag:
        copy.start()
    seat = tp * NY + yi
    xy_ag = [
        remote(norms.at[seat], norms.at[seat], s_xy.at[i], r_xy.at[i], peer)
        for i, peer in enumerate(xy_peers)
    ]
    for copy in xy_ag:
        copy.start()
    for d in range(1, NY):
        src = core * NY + lax.rem(yi + NY - d, NY)
        remote(
            full.at[src], full.at[src], s_y.at[NY - 1 + d - 1], r_y.at[NY - 1 + d - 1], y_peers[d - 1]
        ).wait_recv()
    i = 0
    for dx in range(NX):
        for dy in range(NY):
            if dx or dy:
                src = lax.rem(tp + NX - dx, NX) * NY + lax.rem(yi + NY - dy, NY)
                remote(norms.at[src], norms.at[src], s_xy.at[i], r_xy.at[i], xy_peers[i]).wait_recv()
                i += 1
    total = norms[0]
    for i in range(1, NX * NY):
        total = total + norms[i]
    norm2[core] = total
    core2 = remote(
        full.at[pl.ds(core * NY, NY)], full.at[pl.ds(core * NY, NY)], s_core.at[1], r_core.at[1], twin
    )
    core3 = remote(norm2.at[core], norm2.at[core], s_core.at[2], r_core.at[2], twin)
    core2.start()
    core3.start()
    remote(
        full.at[pl.ds((1 - core) * NY, NY)],
        full.at[pl.ds((1 - core) * NY, NY)],
        s_core.at[1],
        r_core.at[1],
        twin,
    ).wait_recv()
    remote(norm2.at[1 - core], norm2.at[1 - core], s_core.at[2], r_core.at[2], twin).wait_recv()
    norm = jnp.sqrt(norm2[0] + norm2[1])
    scale = (1.0 / jnp.maximum(1.0, norm / CLIP))[0:1, :]
    for j in range(cols):
        for s in range(3):
            gfeat_ref[s, :, pl.ds(j * LANES, LANES)] = scale * full[j, pl.ds(s * 8, TAPS), :]
        gfilt_ref[pl.ds(j * per_col, per_col), :] = scale * full[j, pl.ds(24, per_col), :]

    for copy in halo_copies + [send_prod, send_mid, send_del, core1, core2, core3] + y_rs + z_rs + z_ag + y_ag + xy_ag:
        copy.wait_send()


def local(query_raw, key_raw, value_raw, cotangent, featurizer, filters):
    _, rows, channels = query_raw.shape
    groups = filters.shape[0]
    cols = channels // LANES
    flat = lambda x: x.reshape(rows, channels)
    vmem = pl.BlockSpec(memory_space=pltpu.VMEM)
    grad = jax.ShapeDtypeStruct((rows, channels), BF16)
    dma = pltpu.SemaphoreType.DMA
    pay_rows = 24 + LANES // GROUP
    outs = pl.pallas_call(
        kernel,
        out_shape=(
            grad,
            grad,
            grad,
            jax.ShapeDtypeStruct(featurizer.shape, F32),
            jax.ShapeDtypeStruct(filters.shape, F32),
        ),
        in_specs=[vmem] * 6,
        out_specs=(vmem,) * 5,
        scratch_shapes=[
            pltpu.VMEM((3, HALO, channels), BF16),
            pltpu.VMEM((3, cols, HALO + rows, LANES), F32),
            pltpu.VMEM((cols, rows, LANES), F32),
            pltpu.VMEM((cols, rows, LANES), F32),
            pltpu.VMEM((cols, LAGS + rows, LANES), BF16),
            pltpu.VMEM((cols, LAGS + rows, LANES), BF16),
            pltpu.VMEM((3, cols, rows + 8, LANES), F32),
            pltpu.VMEM((2, groups * BLOCK, LANES), F32),
            pltpu.VMEM((cols, LANES, 2 * LANES), BF16),
            pltpu.VMEM((cols, LANES, 2 * LANES), BF16),
            pltpu.VMEM((3, LANES, LANES), F32),
            pltpu.VMEM((cols, pay_rows, LANES), F32),
            pltpu.VMEM((cols // 2, pay_rows, LANES), F32),
            pltpu.VMEM((NY - 1, pay_rows, LANES), F32),
            pltpu.VMEM((NZ, 2, LANES), F32),
            pltpu.VMEM((NZ - 1, 2, LANES), F32),
            pltpu.VMEM((NZ, 2, LANES), F32),
            pltpu.VMEM((cols, pay_rows, LANES), F32),
            pltpu.VMEM((NX * NY, 8, LANES), F32),
            pltpu.VMEM((2, 8, LANES), F32),
            dma((3,)),
            dma((3,)),
            dma((2,)),
            dma((2,)),
            dma((1,)),
            dma((1,)),
            dma((3,)),
            dma((3,)),
            dma((2 * (NY - 1),)),
            dma((2 * (NY - 1),)),
            dma((2 * (NZ - 1),)),
            dma((2 * (NZ - 1),)),
            dma((NX * NY - 1,)),
            dma((NX * NY - 1,)),
        ],
        compiler_params=pltpu.CompilerParams(
            collective_id=0, has_side_effects=True, vmem_limit_bytes=48 * 1024 * 1024
        ),
        cost_estimate=pl.CostEstimate(
            flops=12 * 256 * rows * channels, bytes_accessed=14 * rows * channels, transcendentals=0
        ),
    )(flat(query_raw), flat(key_raw), flat(value_raw), flat(cotangent), featurizer, filters)
    shape = query_raw.shape
    return (outs[0].reshape(shape), outs[1].reshape(shape), outs[2].reshape(shape), outs[3], outs[4])


def solution(mesh):
    stream = P(None, "ctx", "tp")
    return jax.shard_map(
        local,
        mesh=mesh,
        in_specs=(stream, stream, stream, stream, P(None, None, "tp"), P("tp", None)),
        out_specs=(stream, stream, stream, P(None, None, "tp"), P("tp", None)),
        check_vma=False,
    )
```

```python
import jax
import jax.numpy as jnp
from jax import lax
from jax.experimental import pallas as pl
from jax.experimental.pallas import tpu as pltpu
from jax.sharding import PartitionSpec as P

GROUP = 16
TAPS = 7
LAGS = 128
LANES = 128
HALO = 16
BLOCK = 16
WIN = LAGS + BLOCK
CLIP = 100.0
F32 = jnp.float32
BF16 = jnp.bfloat16
MESH = pl.DeviceIdType.MESH
NY, NZ, NX = 4, 16, 4
TEAM = NY * 4
FAR = NZ // 2
CHUNK = 64


def remote(src, dst, send, recv, device):
    return pltpu.make_async_remote_copy(
        src_ref=src, dst_ref=dst, send_sem=send, recv_sem=recv, device_id=device, device_id_type=MESH
    )


def kernel(
    q_hbm,
    k_hbm,
    v_hbm,
    cot_hbm,
    feat_hbm,
    filt_hbm,
    gq_hbm,
    gk_hbm,
    gv_hbm,
    gfeat_ref,
    gfilt_ref,
    gq_ref,
    gk_ref,
    gv_ref,
    q_ref,
    k_ref,
    v_ref,
    cot_ref,
    feat_ref,
    filt_ref,
    tail,
    ahead_raw,
    raw,
    kfeat,
    vfeat,
    prod,
    mid,
    delta,
    tabs,
    fwd_tab,
    rev_tab,
    pair_sums,
    tap_sums,
    pay,
    got,
    ring,
    full,
    norms,
    s_in,
    s_tail,
    r_tail,
    s_ahead,
    r_ahead,
    s_big,
    r_big,
    s_del,
    r_del,
    s_rs,
    r_rs,
    s_far,
    r_far,
    s_ag,
    r_ag,
    s_norm,
    r_norm,
    s_out,
):
    rows = q_ref.shape[0]
    cols = q_ref.shape[1] // LANES
    per_col = LANES // GROUP
    groups = filt_ref.shape[0]
    half = rows // 2
    ctx = lax.axis_index("ctx")
    tp = lax.axis_index("tp")
    n_ctx = 2 * NY * NZ
    core = lax.rem(ctx, 2)
    zi = lax.rem(lax.div(ctx, 2), NZ)
    yi = lax.div(ctx, 2 * NZ)
    z_low = lax.rem(zi, 2)
    z_far = lax.div(zi, 2)

    def at(x, y, z, c):
        return ((y * NZ + z) * 2 + c, x)

    first = ctx == 0
    last = ctx == n_ctx - 1
    after = (lax.rem(ctx + 1, n_ctx), tp)
    before = (lax.rem(ctx + n_ctx - 1, n_ctx), tp)

    def member(dy, dz, dc, x):
        y = lax.rem(yi + dy, NY)
        zl = lax.rem(z_low + dz, 2)
        c = lax.rem(core + dc, 2)
        return (y * 2 + zl) * 2 + c, at(x, y, z_far * 2 + zl, c)

    steps = [(dy, dz, dc) for dy in range(NY) for dz in range(2) for dc in range(2)]
    me = (yi * 2 + z_low) * 2 + core
    team = [member(dy, dz, dc, tp) for dy, dz, dc in steps[1:]]
    senders = [member((NY - dy) % NY, dz, dc, tp)[0] for dy, dz, dc in steps[1:]]
    wide_team = []
    for dx in range(NX):
        for dy, dz, dc in steps:
            if dx or dy or dz or dc:
                device = member(dy, dz, dc, lax.rem(tp + dx, NX))[1]
                index = member((NY - dy) % NY, dz, dc, tp)[0]
                wide_team.append((device, lax.rem(tp + NX - dx, NX) * TEAM + index))
    far = [at(tp, yi, lax.rem(z_far + d, FAR) * 2 + z_low, core) for d in range(1, FAR)]

    barrier = pltpu.get_barrier_semaphore()
    greeted = [after, before] + far + [device for device, _ in wide_team]
    for peer in greeted:
        pl.semaphore_signal(barrier, inc=1, device_id=peer, device_id_type=MESH)

    loads = [
        pltpu.make_async_copy(src, dst, s_in.at[i])
        for i, (src, dst) in enumerate(
            (
                (feat_hbm, feat_ref),
                (k_hbm, k_ref),
                (v_hbm, v_ref),
                (q_hbm, q_ref),
                (cot_hbm, cot_ref),
                (filt_hbm, filt_ref),
            )
        )
    ]
    for copy in loads:
        copy.start()

    def lanes_of(j):
        return pl.ds(pl.multiple_of(j * LANES, LANES), LANES)

    def weights(s, j):
        return [feat_ref[s, pl.ds(tap, 1), lanes_of(j)] for tap in range(TAPS)]

    def featurized(s, j, taps, start, count):
        total = taps[0] * raw[s, j, pl.ds(HALO + start, count), :]
        for tap in range(1, TAPS):
            total = total + taps[tap] * raw[s, j, pl.ds(HALO + start - tap, count), :]
        return total

    def products(j, spans):
        k_taps, v_taps = weights(1, j), weights(2, j)
        for start, count in spans:
            here = pl.ds(start, count)
            k_here = featurized(1, j, k_taps, start, count)
            v_here = featurized(2, j, v_taps, start, count)
            kfeat[j, here, :] = k_here
            vfeat[j, here, :] = v_here
            prod[j, pl.ds(LAGS + start, count), :] = (k_here * v_here).astype(BF16)

    def mids(j, spans):
        q_taps = weights(0, j)
        for start, count in spans:
            here = pl.ds(start, count)
            q_here = featurized(0, j, q_taps, start, count)
            upstream = cot_ref[here, lanes_of(j)].astype(F32)
            mid[j, here, :] = (upstream * q_here).astype(BF16)

    def widen(s, j, ref):
        raw[s, j, pl.ds(HALO, rows), :] = ref[:, lanes_of(j)].astype(F32)

    low_spans = [(HALO, CHUNK - HALO), (CHUNK, CHUNK)]
    high_spans = [(half, CHUNK), (half + CHUNK, CHUNK)]

    for copy in loads[:3]:
        copy.wait()

    @pl.loop(0, cols)
    def _(j):
        widen(1, j, k_ref)
        widen(2, j, v_ref)
        products(j, high_spans)

    for copy in loads[3:]:
        copy.wait()

    pl.semaphore_wait(barrier, len(greeted))

    tails = [
        remote(ref.at[pl.ds(rows - HALO, HALO), :], tail.at[s], s_tail.at[s], r_tail.at[s], after)
        for s, ref in enumerate((q_ref, k_ref, v_ref))
    ]
    aheads = [
        remote(ref.at[pl.ds(0, HALO), :], ahead_raw.at[i], s_ahead.at[i], r_ahead.at[i], before)
        for i, ref in enumerate((q_ref, cot_ref))
    ]
    send_prod = remote(
        prod.at[:, pl.ds(rows, LAGS), :], prod.at[:, pl.ds(0, LAGS), :], s_big.at[0], r_big.at[0], after
    )
    for copy in tails + aheads + [send_prod]:
        copy.start()

    @pl.loop(0, cols)
    def _(j):
        widen(0, j, q_ref)
        mids(j, low_spans)

    send_mid = remote(
        mid.at[:, pl.ds(HALO, LAGS - HALO), :],
        mid.at[:, pl.ds(rows + HALO, LAGS - HALO), :],
        s_big.at[1],
        r_big.at[1],
        before,
    )
    send_mid.start()

    @pl.loop(0, cols)
    def _(j):
        mids(j, high_spans)
        products(j, low_spans)

    lag_row = lax.broadcasted_iota(jnp.int32, (LAGS, 2 * LANES), 0)
    lag_col = lax.broadcasted_iota(jnp.int32, (LAGS, 2 * LANES), 1)
    flip = jnp.where(lag_row + lag_col == LAGS, 1.0, 0.0).astype(BF16)
    keep = jnp.where(lag_row == lag_col, 1.0, 0.0).astype(BF16)
    for pick, table in ((flip, fwd_tab), (keep, rev_tab)):
        wide = jnp.dot(filt_ref[...], pick, preferred_element_type=F32)
        for b in range(BLOCK):
            moved = pltpu.roll(wide, b, 1) if b else wide
            tabs[0, pl.ds(b, groups, stride=BLOCK), :] = moved[:, :LANES]
            tabs[1, pl.ds(b, groups, stride=BLOCK), :] = moved[:, LANES:]
        for j in range(cols):
            span = pl.ds(j * LANES, LANES)
            table[j] = jnp.concatenate([tabs[0, span, :], tabs[1, span, :]], axis=1).astype(BF16)

    for copy in tails + aheads:
        copy.wait_recv()

    @pl.loop(0, cols)
    def _(j):
        for s in range(3):
            behind = tail[s, :, lanes_of(j)].astype(F32)
            raw[s, j, pl.ds(0, HALO), :] = jnp.where(first, 0.0, behind)
        mids(j, [(0, HALO)])
        products(j, [(0, HALO)])
        raw[0, j, pl.ds(HALO + rows, HALO), :] = ahead_raw[0, :, lanes_of(j)].astype(F32)
        q_next = featurized(0, j, weights(0, j), rows, HALO)
        mid_next = ahead_raw[1, :, lanes_of(j)].astype(F32) * q_next
        mid[j, pl.ds(rows, HALO), :] = jnp.where(last, 0.0, mid_next).astype(BF16)

    lane_group = lax.broadcasted_iota(jnp.int32, (BLOCK, LANES), 1) // GROUP
    row_group = lax.broadcasted_iota(jnp.int32, (LANES, 2 * LANES), 0) // BLOCK
    col_group = lax.rem(lax.broadcasted_iota(jnp.int32, (LANES, 2 * LANES), 1), LANES) // GROUP
    own = jnp.where(row_group == col_group, 1.0, 0.0).astype(BF16)
    quarter = half // 2

    def picked(stacked, lane0):
        out = stacked[0:BLOCK, lane0 : lane0 + LANES]
        for g in range(1, per_col):
            piece = stacked[g * BLOCK : (g + 1) * BLOCK, lane0 : lane0 + LANES]
            out = jnp.where(lane_group == g, piece, out)
        return out

    def window(ref, j, start, count):
        near = ref[j, pl.ds(start, count), :]
        far_rows = ref[j, pl.ds(start + quarter, count), :]
        return jnp.concatenate([near, far_rows], axis=1)

    def add_taps(j, s, acc, d, start):
        out = []
        for tap in range(TAPS):
            moved = raw[s, j, pl.ds(HALO + start - tap, BLOCK), :]
            term = jnp.sum((d * moved).reshape(BLOCK // 8, 8, LANES), axis=0)
            out.append(term if acc is None else acc[tap] + term)
        return out

    def forward(j, base):
        band = fwd_tab[j][:, :WIN]
        acc = None
        for a in range(quarter // BLOCK):
            start = base + a * BLOCK
            stacked = jnp.dot(band, window(prod, j, start, WIN), preferred_element_type=F32)
            for side in range(2):
                here = pl.ds(start + side * quarter, BLOCK)
                upstream = cot_ref[here, lanes_of(j)].astype(F32)
                d = upstream * picked(stacked, side * LANES)
                delta[0, j, here, :] = d
                acc = add_taps(j, 0, acc, d, start + side * quarter)
        return acc

    def backward(j, base):
        band = rev_tab[j][:, :WIN]
        acc_k = None
        acc_v = None
        pairs = jnp.zeros((LANES, WIN), F32)
        for a in range(quarter // BLOCK):
            start = base + a * BLOCK
            ahead = window(mid, j, start, WIN)
            stacked = jnp.dot(band, ahead, preferred_element_type=F32)
            for side in range(2):
                here = pl.ds(start + side * quarter, BLOCK)
                pg = picked(stacked, side * LANES)
                dk = pg * vfeat[j, here, :]
                dv = pg * kfeat[j, here, :]
                delta[1, j, here, :] = dk
                delta[2, j, here, :] = dv
                acc_k = add_taps(j, 1, acc_k, dk, start + side * quarter)
                acc_v = add_taps(j, 2, acc_v, dv, start + side * quarter)
            base_rows = window(prod, j, LAGS + start, BLOCK)
            spread = jnp.concatenate([base_rows] * per_col, axis=0) * own
            pairs = pairs + lax.dot_general(
                spread, ahead, (((1,), (1,)), ((), ())), preferred_element_type=F32
            )
        return acc_k + acc_v, pairs

    @pl.loop(0, cols)
    def _(j):
        acc = forward(j, half)
        more, pairs = backward(j, 0)
        for i, value in enumerate(acc + more):
            tap_sums[j, i] = value
        pair_sums[j, :, :WIN] = pairs

    send_prod.wait_recv()
    send_mid.wait_recv()

    @pl.when(first)
    def _():
        prod[:, pl.ds(0, LAGS), :] = jnp.zeros((cols, LAGS, LANES), BF16)

    @pl.when(last)
    def _():
        mid[:, pl.ds(rows + HALO, LAGS - HALO), :] = jnp.zeros((cols, LAGS - HALO, LANES), BF16)

    @pl.loop(0, cols)
    def _(j):
        acc = forward(j, 0)
        more, pairs = backward(j, half)
        for i, value in enumerate(acc + more):
            row = jnp.sum(tap_sums[j, i] + value, axis=0, keepdims=True)
            s, tap = i // TAPS, i % TAPS
            pay[2 * j + s // 2, pl.ds((s % 2) * 8 + tap, 1), :] = row
        for s in range(3):
            pay[2 * j + s // 2, pl.ds((s % 2) * 8 + TAPS, 1), :] = jnp.zeros((1, LANES), F32)
        pairs = pairs + pair_sums[j, :, :WIN]
        tabs[0, pl.ds(0, LANES), :] = pairs[:, :LANES]
        tabs[1, pl.ds(0, LANES), :BLOCK] = pairs[:, LANES:]
        lags = tabs[0, pl.ds(0, per_col, stride=BLOCK), :]
        for b in range(1, BLOCK):
            low = tabs[0, pl.ds(b, per_col, stride=BLOCK), :]
            high = tabs[1, pl.ds(b, per_col, stride=BLOCK), :]
            both = pltpu.roll(jnp.concatenate([low, high], axis=1), 2 * LANES - b, 1)
            lags = lags + both[:, :LANES]
        pay[2 * j + 1, pl.ds(8, per_col), :] = lags

    scatter = [
        remote(pay.at[index], got.at[i], s_rs.at[i], r_rs.at[i], device)
        for i, (index, device) in enumerate(team)
    ]
    for copy in scatter:
        copy.start()

    send_del = remote(
        delta.at[:, :, pl.ds(0, 8), :], delta.at[:, :, pl.ds(rows, 8), :], s_del.at[0], r_del.at[0], before
    )
    send_del.start()

    def adjoint(s, out_ref, spans):
        @pl.loop(0, cols)
        def _(j):
            taps = weights(s, j)
            for start, count in spans:
                total = taps[0] * delta[s, j, pl.ds(start, count), :]
                for tap in range(1, TAPS):
                    total = total + taps[tap] * delta[s, j, pl.ds(start + tap, count), :]
                out_ref[pl.ds(start, count), lanes_of(j)] = total.astype(BF16)

    body_spans = [(0, CHUNK), (CHUNK, CHUNK), (2 * CHUNK, CHUNK), (3 * CHUNK, CHUNK - HALO)]
    adjoint(0, gq_ref, body_spans)
    adjoint(1, gk_ref, body_spans)
    adjoint(2, gv_ref, body_spans)

    for copy in scatter:
        copy.wait_recv()
    mine = pay[me]
    for i in range(len(team)):
        mine = mine + got[i]
    ring[z_far] = mine
    spread_far = [
        remote(ring.at[z_far], ring.at[z_far], s_far.at[i], r_far.at[i], device)
        for i, device in enumerate(far)
    ]
    for copy in spread_far:
        copy.start()

    send_del.wait_recv()

    @pl.when(last)
    def _():
        delta[:, :, pl.ds(rows, 8), :] = jnp.zeros((3, cols, 8, LANES), F32)

    for s, out_ref in enumerate((gq_ref, gk_ref, gv_ref)):
        adjoint(s, out_ref, [(rows - HALO, HALO)])
    stores = [
        pltpu.make_async_copy(src, dst, s_out.at[i])
        for i, (src, dst) in enumerate(((gq_ref, gq_hbm), (gk_ref, gk_hbm), (gv_ref, gv_hbm)))
    ]
    for copy in stores:
        copy.start()

    for i, device in enumerate(far):
        src = lax.rem(z_far + FAR - 1 - i, FAR)
        remote(ring.at[src], ring.at[src], s_far.at[i], r_far.at[i], device).wait_recv()
    mine = ring[0]
    for i in range(1, FAR):
        mine = mine + ring[i]
    full[me] = mine
    gather = [
        remote(full.at[me], full.at[me], s_ag.at[i], r_ag.at[i], device) for i, (_, device) in enumerate(team)
    ]
    for copy in gather:
        copy.start()
    squares = jnp.sum(jnp.sum(mine * mine, axis=0, keepdims=True), axis=1, keepdims=True)
    seat = tp * TEAM + me
    norms[seat] = jnp.broadcast_to(squares, (1, LANES))
    tell = [
        remote(norms.at[seat], norms.at[seat], s_norm.at[i], r_norm.at[i], device)
        for i, (device, _) in enumerate(wide_team)
    ]
    for copy in tell:
        copy.start()
    for i, (_, device) in enumerate(team):
        remote(full.at[senders[i]], full.at[senders[i]], s_ag.at[i], r_ag.at[i], device).wait_recv()
    for i, (device, src) in enumerate(wide_team):
        remote(norms.at[src], norms.at[src], s_norm.at[i], r_norm.at[i], device).wait_recv()
    total = norms[0]
    for i in range(1, NX * TEAM):
        total = total + norms[i]
    scale = 1.0 / jnp.maximum(1.0, jnp.sqrt(total) / CLIP)
    for j in range(cols):
        for s in range(3):
            gfeat_ref[s, :, pl.ds(j * LANES, LANES)] = scale * full[2 * j + s // 2, pl.ds((s % 2) * 8, TAPS), :]
        gfilt_ref[pl.ds(j * per_col, per_col), :] = scale * full[2 * j + 1, pl.ds(8, per_col), :]

    for copy in tails + aheads + [send_prod, send_mid, send_del] + scatter + spread_far + gather + tell:
        copy.wait_send()
    for copy in stores:
        copy.wait()


def emit(*refs):
    count = 5
    sources, targets, held = refs[:count], refs[count : 2 * count], refs[2 * count : 3 * count]
    s_in, s_out = refs[3 * count :]
    loads = [pltpu.make_async_copy(sources[i], held[i], s_in.at[i]) for i in range(count)]
    stores = [pltpu.make_async_copy(held[i], targets[i], s_out.at[i]) for i in range(count)]
    for copy in loads:
        copy.start()
    for load, store in zip(loads, stores):
        load.wait()
        store.start()
    for copy in stores:
        copy.wait()


def local(query_raw, key_raw, value_raw, cotangent, featurizer, filters):
    _, rows, channels = query_raw.shape
    groups = filters.shape[0]
    cols = channels // LANES
    flat = lambda x: x.reshape(rows, channels)
    vmem = pl.BlockSpec(memory_space=pltpu.VMEM)
    hbm = pl.BlockSpec(memory_space=pltpu.HBM)
    grad = jax.ShapeDtypeStruct((rows, channels), BF16)
    dma = pltpu.SemaphoreType.DMA
    shapes = (
        grad,
        grad,
        grad,
        jax.ShapeDtypeStruct(featurizer.shape, F32),
        jax.ShapeDtypeStruct(filters.shape, F32),
    )
    outs = pl.pallas_call(
        kernel,
        out_shape=shapes,
        in_specs=[hbm] * 6,
        out_specs=(hbm,) * 3 + (vmem,) * 2,
        scratch_shapes=[
            pltpu.VMEM((rows, channels), BF16),
            pltpu.VMEM((rows, channels), BF16),
            pltpu.VMEM((rows, channels), BF16),
            pltpu.VMEM((rows, channels), BF16),
            pltpu.VMEM((rows, channels), BF16),
            pltpu.VMEM((rows, channels), BF16),
            pltpu.VMEM((rows, channels), BF16),
            pltpu.VMEM(featurizer.shape, F32),
            pltpu.VMEM(filters.shape, BF16),
            pltpu.VMEM((3, HALO, channels), BF16),
            pltpu.VMEM((2, HALO, channels), BF16),
            pltpu.VMEM((3, cols, HALO + rows + HALO, LANES), F32),
            pltpu.VMEM((cols, rows, LANES), F32),
            pltpu.VMEM((cols, rows, LANES), F32),
            pltpu.VMEM((cols, LAGS + rows, LANES), BF16),
            pltpu.VMEM((cols, LAGS + rows, LANES), BF16),
            pltpu.VMEM((3, cols, rows + 8, LANES), F32),
            pltpu.VMEM((2, groups * BLOCK, LANES), F32),
            pltpu.VMEM((cols, LANES, 2 * LANES), BF16),
            pltpu.VMEM((cols, LANES, 2 * LANES), BF16),
            pltpu.VMEM((cols, LANES, 2 * LANES), F32),
            pltpu.VMEM((cols, 3 * TAPS, 8, LANES), F32),
            pltpu.VMEM((TEAM, 16, LANES), F32),
            pltpu.VMEM((TEAM - 1, 16, LANES), F32),
            pltpu.VMEM((FAR, 16, LANES), F32),
            pltpu.VMEM((TEAM, 16, LANES), F32),
            pltpu.VMEM((NX * TEAM, 1, LANES), F32),
            dma((6,)),
            dma((3,)),
            dma((3,)),
            dma((2,)),
            dma((2,)),
            dma((2,)),
            dma((2,)),
            dma((1,)),
            dma((1,)),
            dma((TEAM - 1,)),
            dma((TEAM - 1,)),
            dma((FAR - 1,)),
            dma((FAR - 1,)),
            dma((TEAM - 1,)),
            dma((TEAM - 1,)),
            dma((NX * TEAM - 1,)),
            dma((NX * TEAM - 1,)),
            dma((3,)),
        ],
        compiler_params=pltpu.CompilerParams(
            collective_id=0, has_side_effects=True, vmem_limit_bytes=60 * 1024 * 1024
        ),
        cost_estimate=pl.CostEstimate(
            flops=12 * 256 * rows * channels, bytes_accessed=14 * rows * channels, transcendentals=0
        ),
    )(flat(query_raw), flat(key_raw), flat(value_raw), flat(cotangent), featurizer, filters)
    outs = pl.pallas_call(
        emit,
        out_shape=shapes,
        in_specs=[hbm] * 5,
        out_specs=(hbm,) * 5,
        scratch_shapes=[pltpu.VMEM(shape.shape, shape.dtype) for shape in shapes] + [dma((5,)), dma((5,))],
        compiler_params=pltpu.CompilerParams(vmem_limit_bytes=60 * 1024 * 1024),
    )(*outs)
    shape = query_raw.shape
    return (outs[0].reshape(shape), outs[1].reshape(shape), outs[2].reshape(shape), outs[3], outs[4])


def solution(mesh):
    stream = P(None, "ctx", "tp")
    return jax.shard_map(
        local,
        mesh=mesh,
        in_specs=(stream, stream, stream, stream, P(None, None, "tp"), P("tp", None)),
        out_specs=(stream, stream, stream, P(None, None, "tp"), P("tp", None)),
        check_vma=False,
    )
```

```python
import jax
import jax.numpy as jnp
from jax import lax
from jax.experimental import pallas as pl
from jax.experimental.pallas import tpu as pltpu
from jax.sharding import PartitionSpec as P

GROUP = 16
TAPS = 7
LAGS = 128
LANES = 128
HALO = 16
BLOCK = 16
WIN = LAGS + BLOCK
CLIP = 100.0
F32 = jnp.float32
BF16 = jnp.bfloat16
MESH = pl.DeviceIdType.MESH
NY, NZ, NX = 4, 16, 4
TEAM = NY * 4
FAR = NZ // 2
CHUNK = 64


def remote(src, dst, send, recv, device):
    return pltpu.make_async_remote_copy(
        src_ref=src, dst_ref=dst, send_sem=send, recv_sem=recv, device_id=device, device_id_type=MESH
    )


def kernel(
    q_hbm,
    k_hbm,
    v_hbm,
    cot_hbm,
    feat_hbm,
    filt_hbm,
    gq_hbm,
    gk_hbm,
    gv_hbm,
    gfeat_ref,
    gfilt_ref,
    gq_ref,
    gk_ref,
    gv_ref,
    q_ref,
    k_ref,
    v_ref,
    cot_ref,
    feat_ref,
    filt_ref,
    tail,
    ahead_raw,
    raw,
    kfeat,
    vfeat,
    prod,
    mid,
    delta,
    tabs,
    fwd_tab,
    rev_tab,
    pair_sums,
    tap_sums,
    pay,
    got,
    ring,
    full,
    norms,
    s_in,
    s_tail,
    r_tail,
    s_ahead,
    r_ahead,
    s_prod,
    r_prod,
    s_mid,
    r_mid,
    s_del,
    r_del,
    s_rs,
    r_rs,
    s_far,
    r_far,
    s_ag,
    r_ag,
    s_norm,
    r_norm,
    s_out,
    hear,
):
    rows = q_ref.shape[0]
    cols = q_ref.shape[1] // LANES
    per_col = LANES // GROUP
    groups = filt_ref.shape[0]
    half = rows // 2
    ctx = lax.axis_index("ctx")
    tp = lax.axis_index("tp")
    n_ctx = 2 * NY * NZ
    core = lax.rem(ctx, 2)
    zi = lax.rem(lax.div(ctx, 2), NZ)
    yi = lax.div(ctx, 2 * NZ)
    z_low = lax.rem(zi, 2)
    z_far = lax.div(zi, 2)

    def at(x, y, z, c):
        return ((y * NZ + z) * 2 + c, x)

    first = ctx == 0
    last = ctx == n_ctx - 1
    after = (lax.rem(ctx + 1, n_ctx), tp)
    before = (lax.rem(ctx + n_ctx - 1, n_ctx), tp)

    def member(dy, dz, dc, x):
        y = lax.rem(yi + dy, NY)
        zl = lax.rem(z_low + dz, 2)
        c = lax.rem(core + dc, 2)
        return (y * 2 + zl) * 2 + c, at(x, y, z_far * 2 + zl, c)

    steps = [(dy, dz, dc) for dy in range(NY) for dz in range(2) for dc in range(2)]
    me = (yi * 2 + z_low) * 2 + core
    team = [member(dy, dz, dc, tp) for dy, dz, dc in steps[1:]]
    senders = [member((NY - dy) % NY, dz, dc, tp)[0] for dy, dz, dc in steps[1:]]
    wide_team = []
    for dx in range(NX):
        for dy, dz, dc in steps:
            if dx or dy or dz or dc:
                device = member(dy, dz, dc, lax.rem(tp + dx, NX))[1]
                index = member((NY - dy) % NY, dz, dc, tp)[0]
                wide_team.append((device, lax.rem(tp + NX - dx, NX) * TEAM + index))
    far = [at(tp, yi, lax.rem(z_far + d, FAR) * 2 + z_low, core) for d in range(1, FAR)]

    barrier = pltpu.get_barrier_semaphore()
    x_peers = [at(lax.rem(tp + d, NX), yi, zi, core) for d in range(1, NX)]
    z_two = [at(tp, yi, lax.rem(zi + d, NZ), core) for d in (2, NZ - 2)]
    z_four = [at(tp, yi, lax.rem(zi + d, NZ), core) for d in (4, NZ - 4)]
    greeted = [after, before] + [device for _, device in team] + x_peers + z_two
    for peer in greeted:
        pl.semaphore_signal(barrier, inc=1, device_id=peer, device_id_type=MESH)

    loads = [
        pltpu.make_async_copy(src, dst, s_in.at[i])
        for i, (src, dst) in enumerate(
            (
                (feat_hbm, feat_ref),
                (k_hbm, k_ref),
                (v_hbm, v_ref),
                (q_hbm, q_ref),
                (cot_hbm, cot_ref),
                (filt_hbm, filt_ref),
            )
        )
    ]
    for copy in loads:
        copy.start()

    def lanes_of(j):
        return pl.ds(pl.multiple_of(j * LANES, LANES), LANES)

    def weights(s, j):
        return [feat_ref[s, pl.ds(tap, 1), lanes_of(j)] for tap in range(TAPS)]

    def featurized(s, j, taps, start, count):
        total = taps[0] * raw[s, j, pl.ds(HALO + start, count), :]
        for tap in range(1, TAPS):
            total = total + taps[tap] * raw[s, j, pl.ds(HALO + start - tap, count), :]
        return total

    def products(j, spans):
        k_taps, v_taps = weights(1, j), weights(2, j)
        for start, count in spans:
            here = pl.ds(start, count)
            k_here = featurized(1, j, k_taps, start, count)
            v_here = featurized(2, j, v_taps, start, count)
            kfeat[j, here, :] = k_here
            vfeat[j, here, :] = v_here
            prod[j, pl.ds(LAGS + start, count), :] = (k_here * v_here).astype(BF16)

    def mids(j, spans):
        q_taps = weights(0, j)
        for start, count in spans:
            here = pl.ds(start, count)
            q_here = featurized(0, j, q_taps, start, count)
            upstream = cot_ref[here, lanes_of(j)].astype(F32)
            mid[j, here, :] = (upstream * q_here).astype(BF16)

    def widen(s, j, ref):
        raw[s, j, pl.ds(HALO, rows), :] = ref[:, lanes_of(j)].astype(F32)

    low_spans = [(HALO, CHUNK - HALO), (CHUNK, CHUNK)]
    high_spans = [(half, CHUNK), (half + CHUNK, CHUNK)]

    for copy in loads[:3]:
        copy.wait()

    @pl.loop(0, cols)
    def _(j):
        widen(1, j, k_ref)
        widen(2, j, v_ref)
        products(j, high_spans)

    for copy in loads[3:]:
        copy.wait()

    pl.semaphore_wait(barrier, len(greeted))

    for peer in x_peers + z_two:
        pl.semaphore_signal(hear.at[0], inc=1, device_id=peer, device_id_type=MESH)

    tails = [
        remote(ref.at[pl.ds(rows - HALO, HALO), :], tail.at[s], s_tail.at[s], r_tail.at[s], after)
        for s, ref in enumerate((q_ref, k_ref, v_ref))
    ]
    aheads = [
        remote(ref.at[pl.ds(0, HALO), :], ahead_raw.at[i], s_ahead.at[i], r_ahead.at[i], before)
        for i, ref in enumerate((q_ref, cot_ref))
    ]
    for copy in tails + aheads:
        copy.start()

    def prod_copy(j):
        return remote(
            prod.at[j, pl.ds(rows, LAGS), :], prod.at[j, pl.ds(0, LAGS), :], s_prod.at[j], r_prod.at[j], after
        )

    def mid_copy(j):
        return remote(
            mid.at[j, pl.ds(HALO, LAGS - HALO), :],
            mid.at[j, pl.ds(rows + HALO, LAGS - HALO), :],
            s_mid.at[j],
            r_mid.at[j],
            before,
        )

    @pl.loop(0, cols)
    def _(j):
        prod_copy(j).start()

    @pl.loop(0, cols)
    def _(j):
        widen(0, j, q_ref)
        mids(j, low_spans)
        mid_copy(j).start()

    @pl.loop(0, cols)
    def _(j):
        mids(j, high_spans)
        products(j, low_spans)

    lag_row = lax.broadcasted_iota(jnp.int32, (LAGS, 2 * LANES), 0)
    lag_col = lax.broadcasted_iota(jnp.int32, (LAGS, 2 * LANES), 1)
    flip = jnp.where(lag_row + lag_col == LAGS, 1.0, 0.0).astype(BF16)
    keep = jnp.where(lag_row == lag_col, 1.0, 0.0).astype(BF16)
    for pick, table in ((flip, fwd_tab), (keep, rev_tab)):
        wide = jnp.dot(filt_ref[...], pick, preferred_element_type=F32)
        for b in range(BLOCK):
            moved = pltpu.roll(wide, b, 1) if b else wide
            tabs[0, pl.ds(b, groups, stride=BLOCK), :] = moved[:, :LANES]
            tabs[1, pl.ds(b, groups, stride=BLOCK), :] = moved[:, LANES:]
        for j in range(cols):
            span = pl.ds(j * LANES, LANES)
            table[j] = jnp.concatenate([tabs[0, span, :], tabs[1, span, :]], axis=1).astype(BF16)

    for copy in tails + aheads:
        copy.wait_recv()

    @pl.loop(0, cols)
    def _(j):
        for s in range(3):
            behind = tail[s, :, lanes_of(j)].astype(F32)
            raw[s, j, pl.ds(0, HALO), :] = jnp.where(first, 0.0, behind)
        mids(j, [(0, HALO)])
        products(j, [(0, HALO)])
        raw[0, j, pl.ds(HALO + rows, HALO), :] = ahead_raw[0, :, lanes_of(j)].astype(F32)
        q_next = featurized(0, j, weights(0, j), rows, HALO)
        mid_next = ahead_raw[1, :, lanes_of(j)].astype(F32) * q_next
        mid[j, pl.ds(rows, HALO), :] = jnp.where(last, 0.0, mid_next).astype(BF16)

    lane_group = lax.broadcasted_iota(jnp.int32, (BLOCK, LANES), 1) // GROUP
    row_group = lax.broadcasted_iota(jnp.int32, (LANES, 2 * LANES), 0) // BLOCK
    col_group = lax.rem(lax.broadcasted_iota(jnp.int32, (LANES, 2 * LANES), 1), LANES) // GROUP
    own = jnp.where(row_group == col_group, 1.0, 0.0).astype(BF16)
    quarter = half // 2

    def picked(stacked, lane0):
        out = stacked[0:BLOCK, lane0 : lane0 + LANES]
        for g in range(1, per_col):
            piece = stacked[g * BLOCK : (g + 1) * BLOCK, lane0 : lane0 + LANES]
            out = jnp.where(lane_group == g, piece, out)
        return out

    def window(ref, j, start, count):
        near = ref[j, pl.ds(start, count), :]
        far_rows = ref[j, pl.ds(start + quarter, count), :]
        return jnp.concatenate([near, far_rows], axis=1)

    def add_taps(j, s, acc, d, start):
        out = []
        for tap in range(TAPS):
            moved = raw[s, j, pl.ds(HALO + start - tap, BLOCK), :]
            term = jnp.sum((d * moved).reshape(BLOCK // 8, 8, LANES), axis=0)
            out.append(term if acc is None else acc[tap] + term)
        return out

    def forward(j, base):
        band = fwd_tab[j][:, :WIN]
        acc = None
        for a in range(quarter // BLOCK):
            start = base + a * BLOCK
            stacked = jnp.dot(band, window(prod, j, start, WIN), preferred_element_type=F32)
            for side in range(2):
                here = pl.ds(start + side * quarter, BLOCK)
                upstream = cot_ref[here, lanes_of(j)].astype(F32)
                d = upstream * picked(stacked, side * LANES)
                delta[0, j, here, :] = d
                acc = add_taps(j, 0, acc, d, start + side * quarter)
        return acc

    def backward(j, base):
        band = rev_tab[j][:, :WIN]
        acc_k = None
        acc_v = None
        pairs = jnp.zeros((LANES, WIN), F32)
        for a in range(quarter // BLOCK):
            start = base + a * BLOCK
            ahead = window(mid, j, start, WIN)
            stacked = jnp.dot(band, ahead, preferred_element_type=F32)
            for side in range(2):
                here = pl.ds(start + side * quarter, BLOCK)
                pg = picked(stacked, side * LANES)
                dk = pg * vfeat[j, here, :]
                dv = pg * kfeat[j, here, :]
                delta[1, j, here, :] = dk
                delta[2, j, here, :] = dv
                acc_k = add_taps(j, 1, acc_k, dk, start + side * quarter)
                acc_v = add_taps(j, 2, acc_v, dv, start + side * quarter)
            base_rows = window(prod, j, LAGS + start, BLOCK)
            spread = jnp.concatenate([base_rows] * per_col, axis=0) * own
            pairs = pairs + lax.dot_general(
                spread, ahead, (((1,), (1,)), ((), ())), preferred_element_type=F32
            )
        return acc_k + acc_v, pairs

    @pl.loop(0, cols)
    def _(j):
        acc = forward(j, half)
        more, pairs = backward(j, 0)
        for i, value in enumerate(acc + more):
            tap_sums[j, i] = value
        pair_sums[j, :, :WIN] = pairs

    pl.semaphore_wait(hear.at[0], len(x_peers + z_two))
    for peer in z_four:
        pl.semaphore_signal(hear.at[1], inc=1, device_id=peer, device_id_type=MESH)

    @pl.loop(0, cols)
    def _(j):
        prod_copy(j).wait_recv()
        mid_copy(j).wait_recv()

        @pl.when(first)
        def _():
            prod[j, pl.ds(0, LAGS), :] = jnp.zeros((LAGS, LANES), BF16)

        @pl.when(last)
        def _():
            mid[j, pl.ds(rows + HALO, LAGS - HALO), :] = jnp.zeros((LAGS - HALO, LANES), BF16)

        acc = forward(j, 0)
        more, pairs = backward(j, half)
        for i, value in enumerate(acc + more):
            row = jnp.sum(tap_sums[j, i] + value, axis=0, keepdims=True)
            s, tap = i // TAPS, i % TAPS
            pay[2 * j + s // 2, pl.ds((s % 2) * 8 + tap, 1), :] = row
        for s in range(3):
            pay[2 * j + s // 2, pl.ds((s % 2) * 8 + TAPS, 1), :] = jnp.zeros((1, LANES), F32)
        pairs = pairs + pair_sums[j, :, :WIN]
        tabs[0, pl.ds(0, LANES), :] = pairs[:, :LANES]
        tabs[1, pl.ds(0, LANES), :BLOCK] = pairs[:, LANES:]
        lags = tabs[0, pl.ds(0, per_col, stride=BLOCK), :]
        for b in range(1, BLOCK):
            low = tabs[0, pl.ds(b, per_col, stride=BLOCK), :]
            high = tabs[1, pl.ds(b, per_col, stride=BLOCK), :]
            both = pltpu.roll(jnp.concatenate([low, high], axis=1), 2 * LANES - b, 1)
            lags = lags + both[:, :LANES]
        pay[2 * j + 1, pl.ds(8, per_col), :] = lags

    scatter = [
        remote(pay.at[index], got.at[i], s_rs.at[i], r_rs.at[i], device)
        for i, (index, device) in enumerate(team)
    ]
    for copy in scatter:
        copy.start()

    send_del = remote(
        delta.at[:, :, pl.ds(0, 8), :], delta.at[:, :, pl.ds(rows, 8), :], s_del.at[0], r_del.at[0], before
    )
    send_del.start()

    def adjoint(s, out_ref, spans):
        @pl.loop(0, cols)
        def _(j):
            taps = weights(s, j)
            for start, count in spans:
                total = taps[0] * delta[s, j, pl.ds(start, count), :]
                for tap in range(1, TAPS):
                    total = total + taps[tap] * delta[s, j, pl.ds(start + tap, count), :]
                out_ref[pl.ds(start, count), lanes_of(j)] = total.astype(BF16)

    body_spans = [(0, CHUNK), (CHUNK, CHUNK), (2 * CHUNK, CHUNK), (3 * CHUNK, CHUNK - HALO)]
    adjoint(0, gq_ref, body_spans)
    adjoint(1, gk_ref, body_spans)
    adjoint(2, gv_ref, body_spans)

    for copy in scatter:
        copy.wait_recv()
    mine = pay[me]
    for i in range(len(team)):
        mine = mine + got[i]
    ring[z_far] = mine
    spread_far = [
        remote(ring.at[z_far], ring.at[z_far], s_far.at[i], r_far.at[i], device)
        for i, device in enumerate(far)
    ]
    pl.semaphore_wait(hear.at[1], len(z_four))
    for copy in spread_far:
        copy.start()

    send_del.wait_recv()

    @pl.when(last)
    def _():
        delta[:, :, pl.ds(rows, 8), :] = jnp.zeros((3, cols, 8, LANES), F32)

    for s, out_ref in enumerate((gq_ref, gk_ref, gv_ref)):
        adjoint(s, out_ref, [(rows - HALO, HALO)])
    stores = [
        pltpu.make_async_copy(src, dst, s_out.at[i])
        for i, (src, dst) in enumerate(((gq_ref, gq_hbm), (gk_ref, gk_hbm), (gv_ref, gv_hbm)))
    ]
    for copy in stores:
        copy.start()

    for i, device in enumerate(far):
        src = lax.rem(z_far + FAR - 1 - i, FAR)
        remote(ring.at[src], ring.at[src], s_far.at[i], r_far.at[i], device).wait_recv()
    mine = ring[0]
    for i in range(1, FAR):
        mine = mine + ring[i]
    full[me] = mine
    gather = [
        remote(full.at[me], full.at[me], s_ag.at[i], r_ag.at[i], device) for i, (_, device) in enumerate(team)
    ]
    for copy in gather:
        copy.start()
    squares = jnp.sum(jnp.sum(mine * mine, axis=0, keepdims=True), axis=1, keepdims=True)
    seat = tp * TEAM + me
    norms[seat] = jnp.broadcast_to(squares, (1, LANES))
    tell = [
        remote(norms.at[seat], norms.at[seat], s_norm.at[i], r_norm.at[i], device)
        for i, (device, _) in enumerate(wide_team)
    ]
    for copy in tell:
        copy.start()
    for i, (_, device) in enumerate(team):
        remote(full.at[senders[i]], full.at[senders[i]], s_ag.at[i], r_ag.at[i], device).wait_recv()
    for i, (device, src) in enumerate(wide_team):
        remote(norms.at[src], norms.at[src], s_norm.at[i], r_norm.at[i], device).wait_recv()
    total = norms[0]
    for i in range(1, NX * TEAM):
        total = total + norms[i]
    scale = 1.0 / jnp.maximum(1.0, jnp.sqrt(total) / CLIP)
    for j in range(cols):
        for s in range(3):
            gfeat_ref[s, :, pl.ds(j * LANES, LANES)] = scale * full[2 * j + s // 2, pl.ds((s % 2) * 8, TAPS), :]
        gfilt_ref[pl.ds(j * per_col, per_col), :] = scale * full[2 * j + 1, pl.ds(8, per_col), :]

    @pl.loop(0, cols)
    def _(j):
        prod_copy(j).wait_send()
        mid_copy(j).wait_send()

    for copy in tails + aheads + [send_del] + scatter + spread_far + gather + tell:
        copy.wait_send()
    for copy in stores:
        copy.wait()


def emit(*refs):
    count = 5
    sources, targets, held = refs[:count], refs[count : 2 * count], refs[2 * count : 3 * count]
    s_in, s_out = refs[3 * count :]
    loads = [pltpu.make_async_copy(sources[i], held[i], s_in.at[i]) for i in range(count)]
    stores = [pltpu.make_async_copy(held[i], targets[i], s_out.at[i]) for i in range(count)]
    for copy in loads:
        copy.start()
    for load, store in zip(loads, stores):
        load.wait()
        store.start()
    for copy in stores:
        copy.wait()


def local(query_raw, key_raw, value_raw, cotangent, featurizer, filters):
    _, rows, channels = query_raw.shape
    groups = filters.shape[0]
    cols = channels // LANES
    flat = lambda x: x.reshape(rows, channels)
    vmem = pl.BlockSpec(memory_space=pltpu.VMEM)
    hbm = pl.BlockSpec(memory_space=pltpu.HBM)
    grad = jax.ShapeDtypeStruct((rows, channels), BF16)
    dma = pltpu.SemaphoreType.DMA
    shapes = (
        grad,
        grad,
        grad,
        jax.ShapeDtypeStruct(featurizer.shape, F32),
        jax.ShapeDtypeStruct(filters.shape, F32),
    )
    outs = pl.pallas_call(
        kernel,
        out_shape=shapes,
        in_specs=[hbm] * 6,
        out_specs=(hbm,) * 3 + (vmem,) * 2,
        scratch_shapes=[
            pltpu.VMEM((rows, channels), BF16),
            pltpu.VMEM((rows, channels), BF16),
            pltpu.VMEM((rows, channels), BF16),
            pltpu.VMEM((rows, channels), BF16),
            pltpu.VMEM((rows, channels), BF16),
            pltpu.VMEM((rows, channels), BF16),
            pltpu.VMEM((rows, channels), BF16),
            pltpu.VMEM(featurizer.shape, F32),
            pltpu.VMEM(filters.shape, BF16),
            pltpu.VMEM((3, HALO, channels), BF16),
            pltpu.VMEM((2, HALO, channels), BF16),
            pltpu.VMEM((3, cols, HALO + rows + HALO, LANES), F32),
            pltpu.VMEM((cols, rows, LANES), F32),
            pltpu.VMEM((cols, rows, LANES), F32),
            pltpu.VMEM((cols, LAGS + rows, LANES), BF16),
            pltpu.VMEM((cols, LAGS + rows, LANES), BF16),
            pltpu.VMEM((3, cols, rows + 8, LANES), F32),
            pltpu.VMEM((2, groups * BLOCK, LANES), F32),
            pltpu.VMEM((cols, LANES, 2 * LANES), BF16),
            pltpu.VMEM((cols, LANES, 2 * LANES), BF16),
            pltpu.VMEM((cols, LANES, 2 * LANES), F32),
            pltpu.VMEM((cols, 3 * TAPS, 8, LANES), F32),
            pltpu.VMEM((TEAM, 16, LANES), F32),
            pltpu.VMEM((TEAM - 1, 16, LANES), F32),
            pltpu.VMEM((FAR, 16, LANES), F32),
            pltpu.VMEM((TEAM, 16, LANES), F32),
            pltpu.VMEM((NX * TEAM, 1, LANES), F32),
            dma((6,)),
            dma((3,)),
            dma((3,)),
            dma((2,)),
            dma((2,)),
            dma((cols,)),
            dma((cols,)),
            dma((cols,)),
            dma((cols,)),
            dma((1,)),
            dma((1,)),
            dma((TEAM - 1,)),
            dma((TEAM - 1,)),
            dma((FAR - 1,)),
            dma((FAR - 1,)),
            dma((TEAM - 1,)),
            dma((TEAM - 1,)),
            dma((NX * TEAM - 1,)),
            dma((NX * TEAM - 1,)),
            dma((3,)),
            pltpu.SemaphoreType.REGULAR((2,)),
        ],
        compiler_params=pltpu.CompilerParams(
            collective_id=0, has_side_effects=True, vmem_limit_bytes=60 * 1024 * 1024
        ),
        cost_estimate=pl.CostEstimate(
            flops=12 * 256 * rows * channels, bytes_accessed=14 * rows * channels, transcendentals=0
        ),
    )(flat(query_raw), flat(key_raw), flat(value_raw), flat(cotangent), featurizer, filters)
    outs = pl.pallas_call(
        emit,
        out_shape=shapes,
        in_specs=[hbm] * 5,
        out_specs=(hbm,) * 5,
        scratch_shapes=[pltpu.VMEM(shape.shape, shape.dtype) for shape in shapes] + [dma((5,)), dma((5,))],
        compiler_params=pltpu.CompilerParams(vmem_limit_bytes=60 * 1024 * 1024),
    )(*outs)
    shape = query_raw.shape
    return (outs[0].reshape(shape), outs[1].reshape(shape), outs[2].reshape(shape), outs[3], outs[4])


def solution(mesh):
    stream = P(None, "ctx", "tp")
    return jax.shard_map(
        local,
        mesh=mesh,
        in_specs=(stream, stream, stream, stream, P(None, None, "tp"), P("tp", None)),
        out_specs=(stream, stream, stream, P(None, None, "tp"), P("tp", None)),
        check_vma=False,
    )
```

```python
import jax
import jax.numpy as jnp
from jax import lax
from jax.experimental import pallas as pl
from jax.experimental.pallas import tpu as pltpu
from jax.sharding import PartitionSpec as P

GROUP = 16
TAPS = 7
LAGS = 128
LANES = 128
HALO = 16
BLOCK = 16
WIN = LAGS + BLOCK
STACK = LANES // GROUP * BLOCK
CLIP = 100.0
F32 = jnp.float32
BF16 = jnp.bfloat16
MESH = pl.DeviceIdType.MESH
NY, NZ, NX = 4, 16, 4
TEAM = NY * 4
FAR = NZ // 2
CHUNK = 64


def remote(src, dst, send, recv, device):
    return pltpu.make_async_remote_copy(
        src_ref=src, dst_ref=dst, send_sem=send, recv_sem=recv, device_id=device, device_id_type=MESH
    )


def added(terms):
    terms = [term.astype(F32) for term in terms]
    while len(terms) > 1:
        terms = [a + b for a, b in zip(terms[::2], terms[1::2])] + terms[len(terms) & ~1 :]
    return terms[0]


def kernel(
    q_hbm,
    k_hbm,
    v_hbm,
    cot_hbm,
    feat_hbm,
    filt_hbm,
    gq_hbm,
    gk_hbm,
    gv_hbm,
    gfeat_ref,
    gfilt_ref,
    gq_ref,
    gk_ref,
    gv_ref,
    q_ref,
    k_ref,
    v_ref,
    cot_ref,
    feat_ref,
    filt_ref,
    tail,
    ahead_raw,
    raw,
    kfeat,
    vfeat,
    prod,
    mid,
    delta,
    tabs,
    fwd_tab,
    rev_tab,
    tap_sums,
    pay,
    got,
    ring,
    full,
    norms,
    s_in,
    s_tail,
    r_tail,
    s_ahead,
    r_ahead,
    s_prod,
    r_prod,
    s_mid,
    r_mid,
    s_del,
    r_del,
    s_rs,
    r_rs,
    s_far,
    r_far,
    s_ag,
    r_ag,
    s_norm,
    r_norm,
    s_out,
    hear,
):
    rows = q_ref.shape[0]
    cols = q_ref.shape[1] // LANES
    per_col = LANES // GROUP
    groups = filt_ref.shape[0]
    half = rows // 2
    ctx = lax.axis_index("ctx")
    tp = lax.axis_index("tp")
    n_ctx = 2 * NY * NZ
    core = lax.rem(ctx, 2)
    zi = lax.rem(lax.div(ctx, 2), NZ)
    yi = lax.div(ctx, 2 * NZ)
    z_low = lax.rem(zi, 2)
    z_far = lax.div(zi, 2)

    def at(x, y, z, c):
        return ((y * NZ + z) * 2 + c, x)

    first = ctx == 0
    last = ctx == n_ctx - 1
    after = (lax.rem(ctx + 1, n_ctx), tp)
    before = (lax.rem(ctx + n_ctx - 1, n_ctx), tp)

    def member(dy, dz, dc, x):
        y = lax.rem(yi + dy, NY)
        zl = lax.rem(z_low + dz, 2)
        c = lax.rem(core + dc, 2)
        return (y * 2 + zl) * 2 + c, at(x, y, z_far * 2 + zl, c)

    steps = [(dy, dz, dc) for dy in range(NY) for dz in range(2) for dc in range(2)]
    me = (yi * 2 + z_low) * 2 + core
    team = [member(dy, dz, dc, tp) for dy, dz, dc in steps[1:]]
    senders = [member((NY - dy) % NY, dz, dc, tp)[0] for dy, dz, dc in steps[1:]]
    wide_team = []
    for dx in range(NX):
        for dy, dz, dc in steps:
            if dx or dy or dz or dc:
                device = member(dy, dz, dc, lax.rem(tp + dx, NX))[1]
                index = member((NY - dy) % NY, dz, dc, tp)[0]
                wide_team.append((device, lax.rem(tp + NX - dx, NX) * TEAM + index))
    far = [at(tp, yi, lax.rem(z_far + d, FAR) * 2 + z_low, core) for d in range(1, FAR)]

    barrier = pltpu.get_barrier_semaphore()
    x_peers = [at(lax.rem(tp + d, NX), yi, zi, core) for d in range(1, NX)]
    z_two = [at(tp, yi, lax.rem(zi + d, NZ), core) for d in (2, NZ - 2)]
    z_four = [at(tp, yi, lax.rem(zi + d, NZ), core) for d in (4, NZ - 4)]
    greeted = [after, before] + [device for _, device in team] + x_peers + z_two
    for peer in greeted:
        pl.semaphore_signal(barrier, inc=1, device_id=peer, device_id_type=MESH)

    loads = [
        pltpu.make_async_copy(src, dst, s_in.at[i])
        for i, (src, dst) in enumerate(
            (
                (filt_hbm, filt_ref),
                (k_hbm, k_ref),
                (v_hbm, v_ref),
                (feat_hbm, feat_ref),
                (q_hbm, q_ref),
                (cot_hbm, cot_ref),
            )
        )
    ]
    for copy in loads:
        copy.start()

    def lanes_of(j):
        return pl.ds(pl.multiple_of(j * LANES, LANES), LANES)

    def weights(s, j):
        return [feat_ref[s, pl.ds(tap, 1), lanes_of(j)] for tap in range(TAPS)]

    def featurized(s, j, taps, start, count):
        total = taps[0] * raw[s, j, pl.ds(HALO + start, count), :]
        for tap in range(1, TAPS):
            total = total + taps[tap] * raw[s, j, pl.ds(HALO + start - tap, count), :]
        return total

    def products(j, spans):
        k_taps, v_taps = weights(1, j), weights(2, j)
        for start, count in spans:
            here = pl.ds(start, count)
            k_here = featurized(1, j, k_taps, start, count)
            v_here = featurized(2, j, v_taps, start, count)
            kfeat[j, here, :] = k_here
            vfeat[j, here, :] = v_here
            prod[j, pl.ds(LAGS + start, count), :] = (k_here * v_here).astype(BF16)

    def mids(j, spans):
        q_taps = weights(0, j)
        for start, count in spans:
            here = pl.ds(start, count)
            q_here = featurized(0, j, q_taps, start, count)
            upstream = cot_ref[here, lanes_of(j)].astype(F32)
            mid[j, here, :] = (upstream * q_here).astype(BF16)

    def widen(s, j, ref):
        raw[s, j, pl.ds(HALO, rows), :] = ref[:, lanes_of(j)].astype(F32)

    low_spans = [(HALO, CHUNK - HALO), (CHUNK, CHUNK)]
    high_spans = [(half, CHUNK), (half + CHUNK, CHUNK)]

    loads[0].wait()

    lag_row = lax.broadcasted_iota(jnp.int32, (LAGS, 2 * LANES), 0)
    lag_col = lax.broadcasted_iota(jnp.int32, (LAGS, 2 * LANES), 1)
    flip = jnp.where(lag_row + lag_col == LAGS, 1.0, 0.0).astype(BF16)
    keep = jnp.where(lag_row == lag_col, 1.0, 0.0).astype(BF16)
    for pick, table in ((flip, fwd_tab), (keep, rev_tab)):
        wide = jnp.dot(filt_ref[...], pick, preferred_element_type=F32)
        for b in range(BLOCK):
            moved = pltpu.roll(wide, b, 1) if b else wide
            tabs[0, pl.ds(b, groups, stride=BLOCK), :] = moved[:, :LANES]
            tabs[1, pl.ds(b, groups, stride=BLOCK), :] = moved[:, LANES:]
        for j in range(cols):
            span = pl.ds(j * STACK, STACK)
            table[j] = jnp.concatenate([tabs[0, span, :], tabs[1, span, :]], axis=1).astype(BF16)

    for copy in loads[1:4]:
        copy.wait()

    @pl.loop(0, cols)
    def _(j):
        widen(1, j, k_ref)
        widen(2, j, v_ref)
        products(j, high_spans)

    for copy in loads[4:]:
        copy.wait()

    pl.semaphore_wait(barrier, len(greeted))

    for peer in x_peers + z_two:
        pl.semaphore_signal(hear.at[0], inc=1, device_id=peer, device_id_type=MESH)

    tails = [
        remote(ref.at[pl.ds(rows - HALO, HALO), :], tail.at[s], s_tail.at[s], r_tail.at[s], after)
        for s, ref in enumerate((q_ref, k_ref, v_ref))
    ]
    aheads = [
        remote(ref.at[pl.ds(0, HALO), :], ahead_raw.at[i], s_ahead.at[i], r_ahead.at[i], before)
        for i, ref in enumerate((q_ref, cot_ref))
    ]
    for copy in tails + aheads:
        copy.start()

    def prod_copy(j):
        return remote(
            prod.at[j, pl.ds(rows, LAGS), :], prod.at[j, pl.ds(0, LAGS), :], s_prod.at[j], r_prod.at[j], after
        )

    def mid_copy(j):
        return remote(
            mid.at[j, pl.ds(HALO, LAGS - HALO), :],
            mid.at[j, pl.ds(rows + HALO, LAGS - HALO), :],
            s_mid.at[j],
            r_mid.at[j],
            before,
        )

    @pl.loop(0, cols)
    def _(j):
        prod_copy(j).start()

    @pl.loop(0, cols)
    def _(j):
        widen(0, j, q_ref)
        mids(j, low_spans)
        mid_copy(j).start()

    @pl.loop(0, cols)
    def _(j):
        mids(j, high_spans)
        products(j, low_spans)

    for copy in tails + aheads:
        copy.wait_recv()

    @pl.loop(0, cols)
    def _(j):
        for s in range(3):
            behind = tail[s, :, lanes_of(j)].astype(F32)
            raw[s, j, pl.ds(0, HALO), :] = jnp.where(first, 0.0, behind)
        mids(j, [(0, HALO)])
        products(j, [(0, HALO)])
        raw[0, j, pl.ds(HALO + rows, HALO), :] = ahead_raw[0, :, lanes_of(j)].astype(F32)
        q_next = featurized(0, j, weights(0, j), rows, HALO)
        mid_next = ahead_raw[1, :, lanes_of(j)].astype(F32) * q_next
        mid[j, pl.ds(rows, HALO), :] = jnp.where(last, 0.0, mid_next).astype(BF16)

    lane_group = lax.broadcasted_iota(jnp.int32, (BLOCK, LANES), 1) // GROUP
    row_group = lax.broadcasted_iota(jnp.int32, (STACK, 2 * LANES), 0) // BLOCK
    col_group = lax.rem(lax.broadcasted_iota(jnp.int32, (STACK, 2 * LANES), 1), LANES) // GROUP
    own = jnp.where(row_group == col_group, 1.0, 0.0).astype(BF16)
    quarter = half // 2

    def picked(stacked, lane0):
        out = stacked[0:BLOCK, lane0 : lane0 + LANES]
        for g in range(1, per_col):
            piece = stacked[g * BLOCK : (g + 1) * BLOCK, lane0 : lane0 + LANES]
            out = jnp.where(lane_group == g, piece, out)
        return out

    def window(ref, j, start, count):
        near = ref[j, pl.ds(start, count), :]
        far_rows = ref[j, pl.ds(start + quarter, count), :]
        return jnp.concatenate([near, far_rows], axis=1)

    def add_taps(j, s, acc, d, start):
        out = []
        for tap in range(TAPS):
            moved = raw[s, j, pl.ds(HALO + start - tap, BLOCK), :]
            term = jnp.sum((d * moved).reshape(BLOCK // 8, 8, LANES), axis=0)
            out.append(term if acc is None else acc[tap] + term)
        return out

    def forward(j, base):
        band = fwd_tab[j][:, :WIN]
        acc = None
        for a in range(quarter // BLOCK):
            start = base + a * BLOCK
            stacked = jnp.dot(band, window(prod, j, start, WIN), preferred_element_type=F32)
            for side in range(2):
                here = pl.ds(start + side * quarter, BLOCK)
                upstream = cot_ref[here, lanes_of(j)].astype(F32)
                d = upstream * picked(stacked, side * LANES)
                delta[0, j, here, :] = d
                acc = add_taps(j, 0, acc, d, start + side * quarter)
        return acc

    def backward(j, base):
        band = rev_tab[j][:, :WIN]
        acc_k = None
        acc_v = None
        pairs = jnp.zeros((STACK, WIN), F32)
        for a in range(quarter // BLOCK):
            start = base + a * BLOCK
            ahead = window(mid, j, start, WIN)
            stacked = jnp.dot(band, ahead, preferred_element_type=F32)
            for side in range(2):
                here = pl.ds(start + side * quarter, BLOCK)
                pg = picked(stacked, side * LANES)
                dk = pg * vfeat[j, here, :]
                dv = pg * kfeat[j, here, :]
                delta[1, j, here, :] = dk
                delta[2, j, here, :] = dv
                acc_k = add_taps(j, 1, acc_k, dk, start + side * quarter)
                acc_v = add_taps(j, 2, acc_v, dv, start + side * quarter)
            base_rows = window(prod, j, LAGS + start, BLOCK)
            spread = jnp.concatenate([base_rows] * per_col, axis=0) * own
            pairs = pairs + lax.dot_general(
                spread, ahead, (((1,), (1,)), ((), ())), preferred_element_type=F32
            )
        return acc_k + acc_v, pairs

    def tap_rows(j, i):
        return pl.ds(pl.multiple_of((j * 24 + i // TAPS * 8 + i % TAPS) * 8, 8), 8)

    def tile_rows(j):
        return pl.ds(pl.multiple_of(j * STACK, STACK), STACK)

    @pl.loop(0, cols, unroll=4)
    def _(j):
        acc = forward(j, half)
        more, pairs = backward(j, 0)
        for i, value in enumerate(acc + more):
            tap_sums[tap_rows(j, i), :] = value
        for s in range(3):
            tap_sums[pl.ds(pl.multiple_of((j * 24 + s * 8 + TAPS) * 8, 8), 8), :] = jnp.zeros((8, LANES), F32)
        tabs[0, tile_rows(j), :] = pairs[:, :LANES]
        tabs[1, tile_rows(j), :BLOCK] = pairs[:, LANES:]

    pl.semaphore_wait(hear.at[0], len(x_peers + z_two))
    for peer in z_four:
        pl.semaphore_signal(hear.at[1], inc=1, device_id=peer, device_id_type=MESH)

    @pl.loop(0, cols, unroll=4)
    def _(j):
        prod_copy(j).wait_recv()
        mid_copy(j).wait_recv()

        @pl.when(first)
        def _():
            prod[j, pl.ds(0, LAGS), :] = jnp.zeros((LAGS, LANES), BF16)

        @pl.when(last)
        def _():
            mid[j, pl.ds(rows + HALO, LAGS - HALO), :] = jnp.zeros((LAGS - HALO, LANES), BF16)

        acc = forward(j, 0)
        more, pairs = backward(j, half)
        for i, value in enumerate(acc + more):
            tap_sums[tap_rows(j, i), :] += value
        tabs[0, tile_rows(j), :] += pairs[:, :LANES]
        tabs[1, tile_rows(j), :BLOCK] += pairs[:, LANES:]

    taps_total = tap_sums[pl.ds(0, cols * 24, stride=8), :]
    for b in range(1, 8):
        taps_total = taps_total + tap_sums[pl.ds(b, cols * 24, stride=8), :]
    lane = lax.broadcasted_iota(jnp.int32, (groups, LANES), 1)
    lags = tabs[0, pl.ds(0, groups, stride=BLOCK), :]
    for b in range(1, BLOCK):
        low = tabs[0, pl.ds(b, groups, stride=BLOCK), :]
        high = tabs[1, pl.ds(b, groups, stride=BLOCK), :]
        lags = lags + pltpu.roll(jnp.where(lane >= b, low, high), LANES - b, 1)
    for j in range(cols):
        pay[2 * j] = taps_total[j * 24 : j * 24 + 16].astype(BF16)
        pay[2 * j + 1] = jnp.concatenate(
            [taps_total[j * 24 + 16 : j * 24 + 24], lags[j * per_col : (j + 1) * per_col]], axis=0
        ).astype(BF16)

    scatter = [
        remote(pay.at[index], got.at[i], s_rs.at[i], r_rs.at[i], device)
        for i, (index, device) in enumerate(team)
    ]
    for copy in scatter:
        copy.start()

    send_del = remote(
        delta.at[:, :, pl.ds(0, 8), :], delta.at[:, :, pl.ds(rows, 8), :], s_del.at[0], r_del.at[0], before
    )
    send_del.start()

    def adjoint(s, out_ref, spans):
        @pl.loop(0, cols)
        def _(j):
            taps = weights(s, j)
            for start, count in spans:
                total = taps[0] * delta[s, j, pl.ds(start, count), :]
                for tap in range(1, TAPS):
                    total = total + taps[tap] * delta[s, j, pl.ds(start + tap, count), :]
                out_ref[pl.ds(start, count), lanes_of(j)] = total.astype(BF16)

    body_spans = [(0, CHUNK), (CHUNK, CHUNK), (2 * CHUNK, CHUNK), (3 * CHUNK, CHUNK - HALO)]
    adjoint(0, gq_ref, body_spans)
    adjoint(1, gk_ref, body_spans)
    adjoint(2, gv_ref, body_spans)

    for copy in scatter:
        copy.wait_recv()
    mine = added([pay[me]] + [got[i] for i in range(len(team))])
    ring[z_far] = mine.astype(BF16)
    spread_far = [
        remote(ring.at[z_far], ring.at[z_far], s_far.at[i], r_far.at[i], device)
        for i, device in enumerate(far)
    ]
    pl.semaphore_wait(hear.at[1], len(z_four))
    for copy in spread_far:
        copy.start()

    send_del.wait_recv()

    @pl.when(last)
    def _():
        delta[:, :, pl.ds(rows, 8), :] = jnp.zeros((3, cols, 8, LANES), F32)

    for s, out_ref in enumerate((gq_ref, gk_ref, gv_ref)):
        adjoint(s, out_ref, [(rows - HALO, HALO)])
    stores = [
        pltpu.make_async_copy(src, dst, s_out.at[i])
        for i, (src, dst) in enumerate(((gq_ref, gq_hbm), (gk_ref, gk_hbm), (gv_ref, gv_hbm)))
    ]
    for copy in stores:
        copy.start()

    for i, device in enumerate(far):
        src = lax.rem(z_far + FAR - 1 - i, FAR)
        remote(ring.at[src], ring.at[src], s_far.at[i], r_far.at[i], device).wait_recv()
    mine = added([ring[i] for i in range(FAR)])
    full[me] = mine.astype(BF16)
    gather = [
        remote(full.at[me], full.at[me], s_ag.at[i], r_ag.at[i], device) for i, (_, device) in enumerate(team)
    ]
    for copy in gather:
        copy.start()
    squares = jnp.sum(jnp.sum(mine * mine, axis=0, keepdims=True), axis=1, keepdims=True)
    seat = tp * TEAM + me
    norms[seat] = jnp.broadcast_to(squares, (1, LANES))
    tell = [
        remote(norms.at[seat], norms.at[seat], s_norm.at[i], r_norm.at[i], device)
        for i, (device, _) in enumerate(wide_team)
    ]
    for copy in tell:
        copy.start()
    for i, (_, device) in enumerate(team):
        remote(full.at[senders[i]], full.at[senders[i]], s_ag.at[i], r_ag.at[i], device).wait_recv()
    for i, (device, src) in enumerate(wide_team):
        remote(norms.at[src], norms.at[src], s_norm.at[i], r_norm.at[i], device).wait_recv()
    total = added([norms[i] for i in range(NX * TEAM)])
    scale = 1.0 / jnp.maximum(1.0, jnp.sqrt(total) / CLIP)
    for j in range(cols):
        for s in range(3):
            part = full[2 * j + s // 2].astype(F32)[(s % 2) * 8 : (s % 2) * 8 + TAPS]
            gfeat_ref[s, :, pl.ds(j * LANES, LANES)] = scale * part
        gfilt_ref[pl.ds(j * per_col, per_col), :] = scale * full[2 * j + 1].astype(F32)[8:]

    @pl.loop(0, cols)
    def _(j):
        prod_copy(j).wait_send()
        mid_copy(j).wait_send()

    for copy in tails + aheads + [send_del] + scatter + spread_far + gather + tell:
        copy.wait_send()
    for copy in stores:
        copy.wait()


def emit(*refs):
    count = 5
    sources, targets, held = refs[:count], refs[count : 2 * count], refs[2 * count : 3 * count]
    s_in, s_out = refs[3 * count :]
    loads = [pltpu.make_async_copy(sources[i], held[i], s_in.at[i]) for i in range(count)]
    stores = [pltpu.make_async_copy(held[i], targets[i], s_out.at[i]) for i in range(count)]
    for copy in loads:
        copy.start()
    for load, store in zip(loads, stores):
        load.wait()
        store.start()
    for copy in stores:
        copy.wait()


def local(query_raw, key_raw, value_raw, cotangent, featurizer, filters):
    _, rows, channels = query_raw.shape
    groups = filters.shape[0]
    cols = channels // LANES
    flat = lambda x: x.reshape(rows, channels)
    vmem = pl.BlockSpec(memory_space=pltpu.VMEM)
    hbm = pl.BlockSpec(memory_space=pltpu.HBM)
    grad = jax.ShapeDtypeStruct((rows, channels), BF16)
    dma = pltpu.SemaphoreType.DMA
    shapes = (
        grad,
        grad,
        grad,
        jax.ShapeDtypeStruct(featurizer.shape, F32),
        jax.ShapeDtypeStruct(filters.shape, F32),
    )
    outs = pl.pallas_call(
        kernel,
        out_shape=shapes,
        in_specs=[hbm] * 6,
        out_specs=(hbm,) * 3 + (vmem,) * 2,
        scratch_shapes=[
            pltpu.VMEM((rows, channels), BF16),
            pltpu.VMEM((rows, channels), BF16),
            pltpu.VMEM((rows, channels), BF16),
            pltpu.VMEM((rows, channels), BF16),
            pltpu.VMEM((rows, channels), BF16),
            pltpu.VMEM((rows, channels), BF16),
            pltpu.VMEM((rows, channels), BF16),
            pltpu.VMEM(featurizer.shape, F32),
            pltpu.VMEM(filters.shape, BF16),
            pltpu.VMEM((3, HALO, channels), BF16),
            pltpu.VMEM((2, HALO, channels), BF16),
            pltpu.VMEM((3, cols, HALO + rows + HALO, LANES), F32),
            pltpu.VMEM((cols, rows, LANES), F32),
            pltpu.VMEM((cols, rows, LANES), F32),
            pltpu.VMEM((cols, LAGS + rows, LANES), BF16),
            pltpu.VMEM((cols, LAGS + rows, LANES), BF16),
            pltpu.VMEM((3, cols, rows + 8, LANES), F32),
            pltpu.VMEM((2, groups * BLOCK, LANES), F32),
            pltpu.VMEM((cols, STACK, 2 * LANES), BF16),
            pltpu.VMEM((cols, STACK, 2 * LANES), BF16),
            pltpu.VMEM((cols * 24 * 8, LANES), F32),
            pltpu.VMEM((TEAM, 16, LANES), BF16),
            pltpu.VMEM((TEAM - 1, 16, LANES), BF16),
            pltpu.VMEM((FAR, 16, LANES), BF16),
            pltpu.VMEM((TEAM, 16, LANES), BF16),
            pltpu.VMEM((NX * TEAM, 1, LANES), F32),
            dma((6,)),
            dma((3,)),
            dma((3,)),
            dma((2,)),
            dma((2,)),
            dma((cols,)),
            dma((cols,)),
            dma((cols,)),
            dma((cols,)),
            dma((1,)),
            dma((1,)),
            dma((TEAM - 1,)),
            dma((TEAM - 1,)),
            dma((FAR - 1,)),
            dma((FAR - 1,)),
            dma((TEAM - 1,)),
            dma((TEAM - 1,)),
            dma((NX * TEAM - 1,)),
            dma((NX * TEAM - 1,)),
            dma((3,)),
            pltpu.SemaphoreType.REGULAR((2,)),
        ],
        compiler_params=pltpu.CompilerParams(
            collective_id=0, has_side_effects=True, vmem_limit_bytes=60 * 1024 * 1024
        ),
        cost_estimate=pl.CostEstimate(
            flops=12 * 256 * rows * channels, bytes_accessed=14 * rows * channels, transcendentals=0
        ),
    )(flat(query_raw), flat(key_raw), flat(value_raw), flat(cotangent), featurizer, filters)
    outs = pl.pallas_call(
        emit,
        out_shape=shapes,
        in_specs=[hbm] * 5,
        out_specs=(hbm,) * 5,
        scratch_shapes=[pltpu.VMEM(shape.shape, shape.dtype) for shape in shapes] + [dma((5,)), dma((5,))],
        compiler_params=pltpu.CompilerParams(vmem_limit_bytes=60 * 1024 * 1024),
    )(*outs)
    shape = query_raw.shape
    return (outs[0].reshape(shape), outs[1].reshape(shape), outs[2].reshape(shape), outs[3], outs[4])


def solution(mesh):
    stream = P(None, "ctx", "tp")
    return jax.shard_map(
        local,
        mesh=mesh,
        in_specs=(stream, stream, stream, stream, P(None, None, "tp"), P("tp", None)),
        out_specs=(stream, stream, stream, P(None, None, "tp"), P("tp", None)),
        check_vma=False,
    )
```

```python
import jax
import jax.numpy as jnp
from jax import lax
from jax.experimental import pallas as pl
from jax.experimental.pallas import tpu as pltpu
from jax.sharding import PartitionSpec as P

GROUP = 16
TAPS = 7
LAGS = 128
LANES = 128
HALO = 16
BLOCK = 16
WIN = LAGS + BLOCK
STACK = LANES // GROUP * BLOCK
CLIP = 100.0
F32 = jnp.float32
BF16 = jnp.bfloat16
MESH = pl.DeviceIdType.MESH
NY, NZ, NX = 4, 16, 4
TEAM = NY * 4
FAR = NZ // 2
CHUNK = 64


def remote(src, dst, send, recv, device):
    return pltpu.make_async_remote_copy(
        src_ref=src, dst_ref=dst, send_sem=send, recv_sem=recv, device_id=device, device_id_type=MESH
    )


def added(terms):
    terms = [term.astype(F32) for term in terms]
    while len(terms) > 1:
        terms = [a + b for a, b in zip(terms[::2], terms[1::2])] + terms[len(terms) & ~1 :]
    return terms[0]


def kernel(
    q_hbm,
    k_hbm,
    v_hbm,
    cot_hbm,
    feat_hbm,
    filt_hbm,
    gq_hbm,
    gk_hbm,
    gv_hbm,
    gfeat_ref,
    gfilt_ref,
    gq_ref,
    gk_ref,
    gv_ref,
    q_ref,
    k_ref,
    v_ref,
    cot_ref,
    feat_ref,
    filt_ref,
    tail,
    ahead_raw,
    raw,
    kfeat,
    vfeat,
    prod,
    mid,
    delta,
    tabs,
    fwd_tab,
    rev_tab,
    tap_sums,
    pay,
    got,
    ring,
    full,
    norms,
    own_norm,
    s_in,
    s_tail,
    r_tail,
    s_ahead,
    r_ahead,
    s_prod,
    r_prod,
    s_mid,
    r_mid,
    s_del,
    r_del,
    s_rs,
    r_rs,
    s_far,
    r_far,
    s_ag,
    r_ag,
    s_norm,
    r_norm,
    s_out,
    hear,
):
    rows = q_ref.shape[0]
    cols = q_ref.shape[1] // LANES
    per_col = LANES // GROUP
    groups = filt_ref.shape[0]
    half = rows // 2
    ctx = lax.axis_index("ctx")
    tp = lax.axis_index("tp")
    n_ctx = 2 * NY * NZ
    core = lax.rem(ctx, 2)
    zi = lax.rem(lax.div(ctx, 2), NZ)
    yi = lax.div(ctx, 2 * NZ)
    z_low = lax.rem(zi, 2)
    z_far = lax.div(zi, 2)

    def at(x, y, z, c):
        return ((y * NZ + z) * 2 + c, x)

    first = ctx == 0
    last = ctx == n_ctx - 1
    after = (lax.rem(ctx + 1, n_ctx), tp)
    before = (lax.rem(ctx + n_ctx - 1, n_ctx), tp)

    def member(dy, dz, dc, x):
        y = lax.rem(yi + dy, NY)
        zl = lax.rem(z_low + dz, 2)
        c = lax.rem(core + dc, 2)
        return (y * 2 + zl) * 2 + c, at(x, y, z_far * 2 + zl, c)

    steps = [(dy, dz, dc) for dy in range(NY) for dz in range(2) for dc in range(2)]
    me = (yi * 2 + z_low) * 2 + core
    team = [member(dy, dz, dc, tp) for dy, dz, dc in steps[1:]]
    senders = [member((NY - dy) % NY, dz, dc, tp)[0] for dy, dz, dc in steps[1:]]
    wide_team = []
    for dx in range(NX):
        for dy, dz, dc in steps:
            if dx:
                device = member(dy, dz, dc, lax.rem(tp + dx, NX))[1]
                index = member((NY - dy) % NY, dz, dc, tp)[0]
                hops = min(dx, NX - dx) + min(dy, NY - dy) + dz
                wide_team.append((hops, device, lax.rem(tp + NX - dx, NX) * TEAM + index))
    wide_team = [entry[1:] for entry in sorted(wide_team, key=lambda entry: -entry[0])]
    far = [at(tp, yi, lax.rem(z_far + d, FAR) * 2 + z_low, core) for d in range(1, FAR)]

    barrier = pltpu.get_barrier_semaphore()
    x_peers = [at(lax.rem(tp + d, NX), yi, zi, core) for d in range(1, NX)]
    z_two = [at(tp, yi, lax.rem(zi + d, NZ), core) for d in (2, NZ - 2)]
    z_four = [at(tp, yi, lax.rem(zi + d, NZ), core) for d in (4, NZ - 4)]
    greeted = [after, before] + [device for _, device in team] + x_peers + z_two
    for peer in greeted:
        pl.semaphore_signal(barrier, inc=1, device_id=peer, device_id_type=MESH)

    loads = [
        pltpu.make_async_copy(src, dst, s_in.at[i])
        for i, (src, dst) in enumerate(
            (
                (filt_hbm, filt_ref),
                (k_hbm, k_ref),
                (v_hbm, v_ref),
                (feat_hbm, feat_ref),
                (q_hbm, q_ref),
                (cot_hbm, cot_ref),
            )
        )
    ]
    for copy in loads:
        copy.start()

    def lanes_of(j):
        return pl.ds(pl.multiple_of(j * LANES, LANES), LANES)

    def weights(s, j):
        return [feat_ref[s, pl.ds(tap, 1), lanes_of(j)] for tap in range(TAPS)]

    def featurized(s, j, taps, start, count):
        total = taps[0] * raw[s, j, pl.ds(HALO + start, count), :]
        for tap in range(1, TAPS):
            total = total + taps[tap] * raw[s, j, pl.ds(HALO + start - tap, count), :]
        return total

    def products(j, spans):
        k_taps, v_taps = weights(1, j), weights(2, j)
        for start, count in spans:
            here = pl.ds(start, count)
            k_here = featurized(1, j, k_taps, start, count)
            v_here = featurized(2, j, v_taps, start, count)
            kfeat[j, here, :] = k_here
            vfeat[j, here, :] = v_here
            prod[j, pl.ds(LAGS + start, count), :] = (k_here * v_here).astype(BF16)

    def mids(j, spans):
        q_taps = weights(0, j)
        for start, count in spans:
            here = pl.ds(start, count)
            q_here = featurized(0, j, q_taps, start, count)
            upstream = cot_ref[here, lanes_of(j)].astype(F32)
            mid[j, here, :] = (upstream * q_here).astype(BF16)

    def widen(s, j, ref):
        raw[s, j, pl.ds(HALO, rows), :] = ref[:, lanes_of(j)].astype(F32)

    low_spans = [(HALO, CHUNK - HALO), (CHUNK, CHUNK)]
    high_spans = [(half, CHUNK), (half + CHUNK, CHUNK)]

    for copy in loads[:4]:
        copy.wait()

    @pl.loop(0, cols)
    def _(j):
        widen(1, j, k_ref)
        widen(2, j, v_ref)
        products(j, high_spans)

    for copy in loads[4:]:
        copy.wait()

    pl.semaphore_wait(barrier, len(greeted))

    for peer in x_peers + z_two:
        pl.semaphore_signal(hear.at[0], inc=1, device_id=peer, device_id_type=MESH)

    tails = [
        remote(ref.at[pl.ds(rows - HALO, HALO), :], tail.at[s], s_tail.at[s], r_tail.at[s], after)
        for s, ref in enumerate((q_ref, k_ref, v_ref))
    ]
    aheads = [
        remote(ref.at[pl.ds(0, HALO), :], ahead_raw.at[i], s_ahead.at[i], r_ahead.at[i], before)
        for i, ref in enumerate((q_ref, cot_ref))
    ]
    for copy in tails + aheads:
        copy.start()

    def prod_copy(j):
        return remote(
            prod.at[j, pl.ds(rows, LAGS), :], prod.at[j, pl.ds(0, LAGS), :], s_prod.at[j], r_prod.at[j], after
        )

    def mid_copy(j):
        return remote(
            mid.at[j, pl.ds(HALO, LAGS - HALO), :],
            mid.at[j, pl.ds(rows + HALO, LAGS - HALO), :],
            s_mid.at[j],
            r_mid.at[j],
            before,
        )

    @pl.loop(0, cols)
    def _(j):
        prod_copy(j).start()

    @pl.loop(0, cols)
    def _(j):
        widen(0, j, q_ref)
        mids(j, low_spans)
        mid_copy(j).start()

    @pl.loop(0, cols)
    def _(j):
        mids(j, high_spans)
        products(j, low_spans)

    lag_row = lax.broadcasted_iota(jnp.int32, (LAGS, 2 * LANES), 0)
    lag_col = lax.broadcasted_iota(jnp.int32, (LAGS, 2 * LANES), 1)
    flip = jnp.where(lag_row + lag_col == LAGS, 1.0, 0.0).astype(BF16)
    keep = jnp.where(lag_row == lag_col, 1.0, 0.0).astype(BF16)
    for pick, table in ((flip, fwd_tab), (keep, rev_tab)):
        wide = jnp.dot(filt_ref[...], pick, preferred_element_type=F32)
        for b in range(BLOCK):
            moved = pltpu.roll(wide, b, 1) if b else wide
            tabs[0, pl.ds(b, groups, stride=BLOCK), :] = moved[:, :LANES]
            tabs[1, pl.ds(b, groups, stride=BLOCK), :] = moved[:, LANES:]
        for j in range(cols):
            span = pl.ds(j * STACK, STACK)
            table[j] = jnp.concatenate([tabs[0, span, :], tabs[1, span, :]], axis=1).astype(BF16)

    for copy in tails + aheads:
        copy.wait_recv()

    @pl.loop(0, cols)
    def _(j):
        for s in range(3):
            behind = tail[s, :, lanes_of(j)].astype(F32)
            raw[s, j, pl.ds(0, HALO), :] = jnp.where(first, 0.0, behind)
        mids(j, [(0, HALO)])
        products(j, [(0, HALO)])
        raw[0, j, pl.ds(HALO + rows, HALO), :] = ahead_raw[0, :, lanes_of(j)].astype(F32)
        q_next = featurized(0, j, weights(0, j), rows, HALO)
        mid_next = ahead_raw[1, :, lanes_of(j)].astype(F32) * q_next
        mid[j, pl.ds(rows, HALO), :] = jnp.where(last, 0.0, mid_next).astype(BF16)

    lane_group = lax.broadcasted_iota(jnp.int32, (BLOCK, LANES), 1) // GROUP
    row_group = lax.broadcasted_iota(jnp.int32, (STACK, 2 * LANES), 0) // BLOCK
    col_group = lax.rem(lax.broadcasted_iota(jnp.int32, (STACK, 2 * LANES), 1), LANES) // GROUP
    own = jnp.where(row_group == col_group, 1.0, 0.0).astype(BF16)
    quarter = half // 2

    def picked(stacked, lane0):
        out = stacked[0:BLOCK, lane0 : lane0 + LANES]
        for g in range(1, per_col):
            piece = stacked[g * BLOCK : (g + 1) * BLOCK, lane0 : lane0 + LANES]
            out = jnp.where(lane_group == g, piece, out)
        return out

    def window(ref, j, start, count):
        near = ref[j, pl.ds(start, count), :]
        far_rows = ref[j, pl.ds(start + quarter, count), :]
        return jnp.concatenate([near, far_rows], axis=1)

    def add_taps(j, s, acc, d, start):
        out = []
        for tap in range(TAPS):
            moved = raw[s, j, pl.ds(HALO + start - tap, BLOCK), :]
            term = jnp.sum((d * moved).reshape(BLOCK // 8, 8, LANES), axis=0)
            out.append(term if acc is None else acc[tap] + term)
        return out

    def forward(j, base):
        band = fwd_tab[j][:, :WIN]
        acc = None
        for a in range(quarter // BLOCK):
            start = base + a * BLOCK
            stacked = jnp.dot(band, window(prod, j, start, WIN), preferred_element_type=F32)
            for side in range(2):
                here = pl.ds(start + side * quarter, BLOCK)
                upstream = cot_ref[here, lanes_of(j)].astype(F32)
                d = upstream * picked(stacked, side * LANES)
                delta[0, j, here, :] = d
                acc = add_taps(j, 0, acc, d, start + side * quarter)
        return acc

    def backward(j, base):
        band = rev_tab[j][:, :WIN]
        acc_k = None
        acc_v = None
        pairs = jnp.zeros((STACK, WIN), F32)
        for a in range(quarter // BLOCK):
            start = base + a * BLOCK
            ahead = window(mid, j, start, WIN)
            stacked = jnp.dot(band, ahead, preferred_element_type=F32)
            for side in range(2):
                here = pl.ds(start + side * quarter, BLOCK)
                pg = picked(stacked, side * LANES)
                dk = pg * vfeat[j, here, :]
                dv = pg * kfeat[j, here, :]
                delta[1, j, here, :] = dk
                delta[2, j, here, :] = dv
                acc_k = add_taps(j, 1, acc_k, dk, start + side * quarter)
                acc_v = add_taps(j, 2, acc_v, dv, start + side * quarter)
            base_rows = window(prod, j, LAGS + start, BLOCK)
            spread = jnp.concatenate([base_rows] * per_col, axis=0) * own
            pairs = pairs + lax.dot_general(
                spread, ahead, (((1,), (1,)), ((), ())), preferred_element_type=F32
            )
        return acc_k + acc_v, pairs

    def tap_rows(j, i):
        return pl.ds(pl.multiple_of((j * 24 + i // TAPS * 8 + i % TAPS) * 8, 8), 8)

    def tile_rows(j):
        return pl.ds(pl.multiple_of(j * STACK, STACK), STACK)

    @pl.loop(0, cols)
    def _(j):
        acc = forward(j, half)
        more, pairs = backward(j, 0)
        for i, value in enumerate(acc + more):
            tap_sums[tap_rows(j, i), :] = value
        for s in range(3):
            tap_sums[pl.ds(pl.multiple_of((j * 24 + s * 8 + TAPS) * 8, 8), 8), :] = jnp.zeros((8, LANES), F32)
        tabs[0, tile_rows(j), :] = pairs[:, :LANES]
        tabs[1, tile_rows(j), :BLOCK] = pairs[:, LANES:]

    pl.semaphore_wait(hear.at[0], len(x_peers + z_two))
    for peer in z_four:
        pl.semaphore_signal(hear.at[1], inc=1, device_id=peer, device_id_type=MESH)

    @pl.loop(0, cols)
    def _(j):
        prod_copy(j).wait_recv()
        mid_copy(j).wait_recv()

        @pl.when(first)
        def _():
            prod[j, pl.ds(0, LAGS), :] = jnp.zeros((LAGS, LANES), BF16)

        @pl.when(last)
        def _():
            mid[j, pl.ds(rows + HALO, LAGS - HALO), :] = jnp.zeros((LAGS - HALO, LANES), BF16)

        acc = forward(j, 0)
        more, pairs = backward(j, half)
        for i, value in enumerate(acc + more):
            tap_sums[tap_rows(j, i), :] += value
        tabs[0, tile_rows(j), :] += pairs[:, :LANES]
        tabs[1, tile_rows(j), :BLOCK] += pairs[:, LANES:]

    taps_total = tap_sums[pl.ds(0, cols * 24, stride=8), :]
    for b in range(1, 8):
        taps_total = taps_total + tap_sums[pl.ds(b, cols * 24, stride=8), :]
    lane = lax.broadcasted_iota(jnp.int32, (groups, LANES), 1)
    lags = tabs[0, pl.ds(0, groups, stride=BLOCK), :]
    for b in range(1, BLOCK):
        low = tabs[0, pl.ds(b, groups, stride=BLOCK), :]
        high = tabs[1, pl.ds(b, groups, stride=BLOCK), :]
        lags = lags + pltpu.roll(jnp.where(lane >= b, low, high), LANES - b, 1)
    for j in range(cols):
        pay[2 * j] = taps_total[j * 24 : j * 24 + 16].astype(BF16)
        pay[2 * j + 1] = jnp.concatenate(
            [taps_total[j * 24 + 16 : j * 24 + 24], lags[j * per_col : (j + 1) * per_col]], axis=0
        ).astype(BF16)

    scatter = [
        remote(pay.at[index], got.at[i], s_rs.at[i], r_rs.at[i], device)
        for i, (index, device) in enumerate(team)
    ]
    for copy in scatter:
        copy.start()

    send_del = remote(
        delta.at[:, :, pl.ds(0, 8), :], delta.at[:, :, pl.ds(rows, 8), :], s_del.at[0], r_del.at[0], before
    )
    send_del.start()

    def adjoint(s, out_ref, spans):
        @pl.loop(0, cols)
        def _(j):
            taps = weights(s, j)
            for start, count in spans:
                total = taps[0] * delta[s, j, pl.ds(start, count), :]
                for tap in range(1, TAPS):
                    total = total + taps[tap] * delta[s, j, pl.ds(start + tap, count), :]
                out_ref[pl.ds(start, count), lanes_of(j)] = total.astype(BF16)

    body_spans = [(0, CHUNK), (CHUNK, CHUNK), (2 * CHUNK, CHUNK), (3 * CHUNK, CHUNK - HALO)]
    adjoint(0, gq_ref, body_spans)
    adjoint(1, gk_ref, body_spans)
    adjoint(2, gv_ref, body_spans)

    for copy in scatter:
        copy.wait_recv()
    mine = added([pay[me]] + [got[i] for i in range(len(team))])
    ring[z_far] = mine.astype(BF16)
    spread_far = [
        remote(ring.at[z_far], ring.at[z_far], s_far.at[i], r_far.at[i], device)
        for i, device in enumerate(far)
    ]
    pl.semaphore_wait(hear.at[1], len(z_four))
    for copy in spread_far:
        copy.start()

    send_del.wait_recv()

    @pl.when(last)
    def _():
        delta[:, :, pl.ds(rows, 8), :] = jnp.zeros((3, cols, 8, LANES), F32)

    for s, out_ref in enumerate((gq_ref, gk_ref, gv_ref)):
        adjoint(s, out_ref, [(rows - HALO, HALO)])
    stores = [
        pltpu.make_async_copy(src, dst, s_out.at[i])
        for i, (src, dst) in enumerate(((gq_ref, gq_hbm), (gk_ref, gk_hbm), (gv_ref, gv_hbm)))
    ]
    for copy in stores:
        copy.start()

    for i, device in enumerate(far):
        src = lax.rem(z_far + FAR - 1 - i, FAR)
        remote(ring.at[src], ring.at[src], s_far.at[i], r_far.at[i], device).wait_recv()
    mine = added([ring[i] for i in range(FAR)])
    full[me] = mine.astype(BF16)

    def squares(index):
        value = full[index].astype(F32)
        total = jnp.sum(jnp.sum(value * value, axis=0, keepdims=True), axis=1, keepdims=True)
        return jnp.broadcast_to(total, (1, LANES))

    seat = tp * TEAM + me
    own_norm[...] = squares(me)
    tell = [
        remote(own_norm, norms.at[seat], s_norm.at[i], r_norm.at[i], device)
        for i, (device, _) in enumerate(wide_team)
    ]
    gather = [
        remote(full.at[me], full.at[me], s_ag.at[i], r_ag.at[i], device) for i, (_, device) in enumerate(team)
    ]
    for copy in tell + gather:
        copy.start()
    for i, (_, device) in enumerate(team):
        remote(full.at[senders[i]], full.at[senders[i]], s_ag.at[i], r_ag.at[i], device).wait_recv()
    for index in range(TEAM):
        norms[tp * TEAM + index] = squares(index)
    for i, (device, src) in enumerate(wide_team):
        remote(norms.at[src], norms.at[src], s_norm.at[i], r_norm.at[i], device).wait_recv()
    total = added([norms[i] for i in range(NX * TEAM)])
    scale = 1.0 / jnp.maximum(1.0, jnp.sqrt(total) / CLIP)
    for j in range(cols):
        for s in range(3):
            part = full[2 * j + s // 2].astype(F32)[(s % 2) * 8 : (s % 2) * 8 + TAPS]
            gfeat_ref[s, :, pl.ds(j * LANES, LANES)] = scale * part
        gfilt_ref[pl.ds(j * per_col, per_col), :] = scale * full[2 * j + 1].astype(F32)[8:]

    @pl.loop(0, cols)
    def _(j):
        prod_copy(j).wait_send()
        mid_copy(j).wait_send()

    for copy in tails + aheads + [send_del] + scatter + spread_far + gather + tell:
        copy.wait_send()
    for copy in stores:
        copy.wait()


def emit(*refs):
    count = 5
    sources, targets, held = refs[:count], refs[count : 2 * count], refs[2 * count : 3 * count]
    s_in, s_out = refs[3 * count :]
    loads = [pltpu.make_async_copy(sources[i], held[i], s_in.at[i]) for i in range(count)]
    stores = [pltpu.make_async_copy(held[i], targets[i], s_out.at[i]) for i in range(count)]
    for copy in loads:
        copy.start()
    for load, store in zip(loads, stores):
        load.wait()
        store.start()
    for copy in stores:
        copy.wait()


def local(query_raw, key_raw, value_raw, cotangent, featurizer, filters):
    _, rows, channels = query_raw.shape
    groups = filters.shape[0]
    cols = channels // LANES
    flat = lambda x: x.reshape(rows, channels)
    vmem = pl.BlockSpec(memory_space=pltpu.VMEM)
    hbm = pl.BlockSpec(memory_space=pltpu.HBM)
    grad = jax.ShapeDtypeStruct((rows, channels), BF16)
    dma = pltpu.SemaphoreType.DMA
    shapes = (
        grad,
        grad,
        grad,
        jax.ShapeDtypeStruct(featurizer.shape, F32),
        jax.ShapeDtypeStruct(filters.shape, F32),
    )
    outs = pl.pallas_call(
        kernel,
        out_shape=shapes,
        in_specs=[hbm] * 6,
        out_specs=(hbm,) * 3 + (vmem,) * 2,
        scratch_shapes=[
            pltpu.VMEM((rows, channels), BF16),
            pltpu.VMEM((rows, channels), BF16),
            pltpu.VMEM((rows, channels), BF16),
            pltpu.VMEM((rows, channels), BF16),
            pltpu.VMEM((rows, channels), BF16),
            pltpu.VMEM((rows, channels), BF16),
            pltpu.VMEM((rows, channels), BF16),
            pltpu.VMEM(featurizer.shape, F32),
            pltpu.VMEM(filters.shape, BF16),
            pltpu.VMEM((3, HALO, channels), BF16),
            pltpu.VMEM((2, HALO, channels), BF16),
            pltpu.VMEM((3, cols, HALO + rows + HALO, LANES), F32),
            pltpu.VMEM((cols, rows, LANES), F32),
            pltpu.VMEM((cols, rows, LANES), F32),
            pltpu.VMEM((cols, LAGS + rows, LANES), BF16),
            pltpu.VMEM((cols, LAGS + rows, LANES), BF16),
            pltpu.VMEM((3, cols, rows + 8, LANES), F32),
            pltpu.VMEM((2, groups * BLOCK, LANES), F32),
            pltpu.VMEM((cols, STACK, 2 * LANES), BF16),
            pltpu.VMEM((cols, STACK, 2 * LANES), BF16),
            pltpu.VMEM((cols * 24 * 8, LANES), F32),
            pltpu.VMEM((TEAM, 16, LANES), BF16),
            pltpu.VMEM((TEAM - 1, 16, LANES), BF16),
            pltpu.VMEM((FAR, 16, LANES), BF16),
            pltpu.VMEM((TEAM, 16, LANES), BF16),
            pltpu.VMEM((NX * TEAM, 1, LANES), F32),
            pltpu.VMEM((1, LANES), F32),
            dma((6,)),
            dma((3,)),
            dma((3,)),
            dma((2,)),
            dma((2,)),
            dma((cols,)),
            dma((cols,)),
            dma((cols,)),
            dma((cols,)),
            dma((1,)),
            dma((1,)),
            dma((TEAM - 1,)),
            dma((TEAM - 1,)),
            dma((FAR - 1,)),
            dma((FAR - 1,)),
            dma((TEAM - 1,)),
            dma((TEAM - 1,)),
            dma(((NX - 1) * TEAM,)),
            dma(((NX - 1) * TEAM,)),
            dma((3,)),
            pltpu.SemaphoreType.REGULAR((2,)),
        ],
        compiler_params=pltpu.CompilerParams(
            collective_id=0, has_side_effects=True, vmem_limit_bytes=60 * 1024 * 1024
        ),
        cost_estimate=pl.CostEstimate(
            flops=12 * 256 * rows * channels, bytes_accessed=14 * rows * channels, transcendentals=0
        ),
    )(flat(query_raw), flat(key_raw), flat(value_raw), flat(cotangent), featurizer, filters)
    outs = pl.pallas_call(
        emit,
        out_shape=shapes,
        in_specs=[hbm] * 5,
        out_specs=(hbm,) * 5,
        scratch_shapes=[pltpu.VMEM(shape.shape, shape.dtype) for shape in shapes] + [dma((5,)), dma((5,))],
        compiler_params=pltpu.CompilerParams(vmem_limit_bytes=60 * 1024 * 1024),
    )(*outs)
    shape = query_raw.shape
    return (outs[0].reshape(shape), outs[1].reshape(shape), outs[2].reshape(shape), outs[3], outs[4])


def solution(mesh):
    stream = P(None, "ctx", "tp")
    return jax.shard_map(
        local,
        mesh=mesh,
        in_specs=(stream, stream, stream, stream, P(None, None, "tp"), P("tp", None)),
        out_specs=(stream, stream, stream, P(None, None, "tp"), P("tp", None)),
        check_vma=False,
    )
```

```python
import jax
import jax.numpy as jnp
from jax import lax
from jax.experimental import pallas as pl
from jax.experimental.pallas import tpu as pltpu
from jax.sharding import PartitionSpec as P

GROUP = 16
TAPS = 7
LAGS = 128
LANES = 128
HALO = 16
BLOCK = 16
WIN = LAGS + BLOCK
STACK = LANES // GROUP * BLOCK
CLIP = 100.0
F32 = jnp.float32
BF16 = jnp.bfloat16
MESH = pl.DeviceIdType.MESH
NY, NZ, NX = 4, 16, 4
TEAM = NY * 4
FAR = NZ // 2
CHUNK = 64


def remote(src, dst, send, recv, device):
    return pltpu.make_async_remote_copy(
        src_ref=src, dst_ref=dst, send_sem=send, recv_sem=recv, device_id=device, device_id_type=MESH
    )


def added(terms):
    terms = [term.astype(F32) for term in terms]
    while len(terms) > 1:
        terms = [a + b for a, b in zip(terms[::2], terms[1::2])] + terms[len(terms) & ~1 :]
    return terms[0]


def kernel(
    q_hbm,
    k_hbm,
    v_hbm,
    cot_hbm,
    feat_hbm,
    filt_hbm,
    gq_hbm,
    gk_hbm,
    gv_hbm,
    gfeat_ref,
    gfilt_ref,
    gq_ref,
    gk_ref,
    gv_ref,
    q_ref,
    k_ref,
    v_ref,
    cot_ref,
    feat_ref,
    filt_ref,
    tail,
    ahead_raw,
    raw,
    kfeat,
    vfeat,
    prod,
    mid,
    delta,
    tabs,
    fwd_tab,
    rev_tab,
    tap_sums,
    pay,
    got,
    ring,
    full,
    norms,
    own_norm,
    s_in,
    s_tail,
    r_tail,
    s_ahead,
    r_ahead,
    s_prod,
    r_prod,
    s_mid,
    r_mid,
    s_del,
    r_del,
    s_rs,
    r_rs,
    s_far,
    r_far,
    s_ag,
    r_ag,
    s_norm,
    r_norm,
    s_out,
    hear,
):
    rows = q_ref.shape[0]
    cols = q_ref.shape[1] // LANES
    per_col = LANES // GROUP
    groups = filt_ref.shape[0]
    half = rows // 2
    ctx = lax.axis_index("ctx")
    tp = lax.axis_index("tp")
    n_ctx = 2 * NY * NZ
    core = lax.rem(ctx, 2)
    zi = lax.rem(lax.div(ctx, 2), NZ)
    yi = lax.div(ctx, 2 * NZ)
    z_low = lax.rem(zi, 2)
    z_far = lax.div(zi, 2)

    def at(x, y, z, c):
        return ((y * NZ + z) * 2 + c, x)

    first = ctx == 0
    last = ctx == n_ctx - 1
    after = (lax.rem(ctx + 1, n_ctx), tp)
    before = (lax.rem(ctx + n_ctx - 1, n_ctx), tp)

    def member(dy, dz, dc, x):
        y = lax.rem(yi + dy, NY)
        zl = lax.rem(z_low + dz, 2)
        c = lax.rem(core + dc, 2)
        return (y * 2 + zl) * 2 + c, at(x, y, z_far * 2 + zl, c)

    steps = [(dy, dz, dc) for dy in range(NY) for dz in range(2) for dc in range(2)]
    me = (yi * 2 + z_low) * 2 + core
    team = [member(dy, dz, dc, tp) for dy, dz, dc in steps[1:]]
    senders = [member((NY - dy) % NY, dz, dc, tp)[0] for dy, dz, dc in steps[1:]]
    wide_team = []
    for dx in range(NX):
        for dy, dz, dc in steps:
            if dx:
                device = member(dy, dz, dc, lax.rem(tp + dx, NX))[1]
                index = member((NY - dy) % NY, dz, dc, tp)[0]
                hops = min(dx, NX - dx) + min(dy, NY - dy) + dz
                wide_team.append((hops, device, lax.rem(tp + NX - dx, NX) * TEAM + index))
    wide_team = [entry[1:] for entry in sorted(wide_team, key=lambda entry: -entry[0])]
    far = [at(tp, yi, lax.rem(z_far + d, FAR) * 2 + z_low, core) for d in range(1, FAR)]

    barrier = pltpu.get_barrier_semaphore()
    x_peers = [at(lax.rem(tp + d, NX), yi, zi, core) for d in range(1, NX)]
    z_two = [at(tp, yi, lax.rem(zi + d, NZ), core) for d in (2, NZ - 2)]
    z_four = [at(tp, yi, lax.rem(zi + d, NZ), core) for d in (4, NZ - 4)]
    greeted = [after, before] + [device for _, device in team] + x_peers + z_two
    for peer in greeted:
        pl.semaphore_signal(barrier, inc=1, device_id=peer, device_id_type=MESH)

    loads = [
        pltpu.make_async_copy(src, dst, s_in.at[i])
        for i, (src, dst) in enumerate(
            (
                (filt_hbm, filt_ref),
                (k_hbm, k_ref),
                (v_hbm, v_ref),
                (feat_hbm, feat_ref),
                (q_hbm, q_ref),
                (cot_hbm, cot_ref),
            )
        )
    ]
    for copy in loads:
        copy.start()

    def lanes_of(j):
        return pl.ds(pl.multiple_of(j * LANES, LANES), LANES)

    def weights(s, j):
        return [feat_ref[s, pl.ds(tap, 1), lanes_of(j)] for tap in range(TAPS)]

    def featurized(s, j, taps, start, count):
        total = taps[0] * raw[s, j, pl.ds(HALO + start, count), :]
        for tap in range(1, TAPS):
            total = total + taps[tap] * raw[s, j, pl.ds(HALO + start - tap, count), :]
        return total

    def products(j, spans):
        k_taps, v_taps = weights(1, j), weights(2, j)
        for start, count in spans:
            here = pl.ds(start, count)
            k_here = featurized(1, j, k_taps, start, count)
            v_here = featurized(2, j, v_taps, start, count)
            kfeat[j, here, :] = k_here
            vfeat[j, here, :] = v_here
            prod[j, pl.ds(LAGS + start, count), :] = (k_here * v_here).astype(BF16)

    def mids(j, spans):
        q_taps = weights(0, j)
        for start, count in spans:
            here = pl.ds(start, count)
            q_here = featurized(0, j, q_taps, start, count)
            upstream = cot_ref[here, lanes_of(j)].astype(F32)
            mid[j, here, :] = (upstream * q_here).astype(BF16)

    def widen(s, j, ref):
        raw[s, j, pl.ds(HALO, rows), :] = ref[:, lanes_of(j)].astype(F32)

    low_spans = [(HALO, CHUNK - HALO), (CHUNK, CHUNK)]
    high_spans = [(half, CHUNK), (half + CHUNK, CHUNK)]

    for copy in loads[:4]:
        copy.wait()

    @pl.loop(0, cols)
    def _(j):
        widen(1, j, k_ref)
        widen(2, j, v_ref)
        products(j, high_spans)

    for copy in loads[4:]:
        copy.wait()

    pl.semaphore_wait(barrier, len(greeted))

    for peer in x_peers + z_two:
        pl.semaphore_signal(hear.at[0], inc=1, device_id=peer, device_id_type=MESH)

    tails = [
        remote(ref.at[pl.ds(rows - HALO, HALO), :], tail.at[s], s_tail.at[s], r_tail.at[s], after)
        for s, ref in enumerate((q_ref, k_ref, v_ref))
    ]
    aheads = [
        remote(ref.at[pl.ds(0, HALO), :], ahead_raw.at[i], s_ahead.at[i], r_ahead.at[i], before)
        for i, ref in enumerate((q_ref, cot_ref))
    ]
    for copy in tails + aheads:
        copy.start()

    def prod_copy(j):
        return remote(
            prod.at[j, pl.ds(rows, LAGS), :], prod.at[j, pl.ds(0, LAGS), :], s_prod.at[j], r_prod.at[j], after
        )

    def mid_copy(j):
        return remote(
            mid.at[j, pl.ds(HALO, LAGS - HALO), :],
            mid.at[j, pl.ds(rows + HALO, LAGS - HALO), :],
            s_mid.at[j],
            r_mid.at[j],
            before,
        )

    @pl.loop(0, cols)
    def _(j):
        prod_copy(j).start()

    @pl.loop(0, cols)
    def _(j):
        widen(0, j, q_ref)
        mids(j, low_spans)
        mid_copy(j).start()

    @pl.loop(0, cols)
    def _(j):
        mids(j, high_spans)
        products(j, low_spans)

    lag_row = lax.broadcasted_iota(jnp.int32, (LAGS, 2 * LANES), 0)
    lag_col = lax.broadcasted_iota(jnp.int32, (LAGS, 2 * LANES), 1)
    flip = jnp.where(lag_row + lag_col == LAGS, 1.0, 0.0).astype(BF16)
    keep = jnp.where(lag_row == lag_col, 1.0, 0.0).astype(BF16)
    for pick, table in ((flip, fwd_tab), (keep, rev_tab)):
        wide = jnp.dot(filt_ref[...], pick, preferred_element_type=F32)
        for b in range(BLOCK):
            moved = pltpu.roll(wide, b, 1) if b else wide
            tabs[0, pl.ds(b, groups, stride=BLOCK), :] = moved[:, :LANES]
            tabs[1, pl.ds(b, groups, stride=BLOCK), :] = moved[:, LANES:]
        for j in range(cols):
            span = pl.ds(j * STACK, STACK)
            table[j] = jnp.concatenate([tabs[0, span, :], tabs[1, span, :]], axis=1).astype(BF16)

    for copy in tails + aheads:
        copy.wait_recv()

    @pl.loop(0, cols)
    def _(j):
        for s in range(3):
            behind = tail[s, :, lanes_of(j)].astype(F32)
            raw[s, j, pl.ds(0, HALO), :] = jnp.where(first, 0.0, behind)
        mids(j, [(0, HALO)])
        products(j, [(0, HALO)])
        raw[0, j, pl.ds(HALO + rows, HALO), :] = ahead_raw[0, :, lanes_of(j)].astype(F32)
        q_next = featurized(0, j, weights(0, j), rows, HALO)
        mid_next = ahead_raw[1, :, lanes_of(j)].astype(F32) * q_next
        mid[j, pl.ds(rows, HALO), :] = jnp.where(last, 0.0, mid_next).astype(BF16)

    lane_group = lax.broadcasted_iota(jnp.int32, (BLOCK, LANES), 1) // GROUP
    row_group = lax.broadcasted_iota(jnp.int32, (STACK, 2 * LANES), 0) // BLOCK
    col_group = lax.rem(lax.broadcasted_iota(jnp.int32, (STACK, 2 * LANES), 1), LANES) // GROUP
    own = jnp.where(row_group == col_group, 1.0, 0.0).astype(BF16)
    quarter = half // 2

    def picked(stacked, lane0):
        out = stacked[0:BLOCK, lane0 : lane0 + LANES]
        for g in range(1, per_col):
            piece = stacked[g * BLOCK : (g + 1) * BLOCK, lane0 : lane0 + LANES]
            out = jnp.where(lane_group == g, piece, out)
        return out

    def window(ref, j, start, count):
        near = ref[j, pl.ds(start, count), :]
        far_rows = ref[j, pl.ds(start + quarter, count), :]
        return jnp.concatenate([near, far_rows], axis=1)

    def add_taps(j, s, acc, d, start):
        out = []
        for tap in range(TAPS):
            moved = raw[s, j, pl.ds(HALO + start - tap, BLOCK), :]
            term = jnp.sum((d * moved).reshape(BLOCK // 8, 8, LANES), axis=0)
            out.append(term if acc is None else acc[tap] + term)
        return out

    def forward(j, base):
        band = fwd_tab[j][:, :WIN]
        acc = None
        for a in range(quarter // BLOCK):
            start = base + a * BLOCK
            stacked = jnp.dot(band, window(prod, j, start, WIN), preferred_element_type=F32)
            for side in range(2):
                here = pl.ds(start + side * quarter, BLOCK)
                upstream = cot_ref[here, lanes_of(j)].astype(F32)
                d = upstream * picked(stacked, side * LANES)
                delta[0, j, here, :] = d
                acc = add_taps(j, 0, acc, d, start + side * quarter)
        return acc

    def backward(j, base):
        band = rev_tab[j][:, :WIN]
        acc_k = None
        acc_v = None
        pairs = jnp.zeros((STACK, WIN), F32)
        for a in range(quarter // BLOCK):
            start = base + a * BLOCK
            ahead = window(mid, j, start, WIN)
            stacked = jnp.dot(band, ahead, preferred_element_type=F32)
            for side in range(2):
                here = pl.ds(start + side * quarter, BLOCK)
                pg = picked(stacked, side * LANES)
                dk = pg * vfeat[j, here, :]
                dv = pg * kfeat[j, here, :]
                delta[1, j, here, :] = dk
                delta[2, j, here, :] = dv
                acc_k = add_taps(j, 1, acc_k, dk, start + side * quarter)
                acc_v = add_taps(j, 2, acc_v, dv, start + side * quarter)
            base_rows = window(prod, j, LAGS + start, BLOCK)
            spread = jnp.concatenate([base_rows] * per_col, axis=0) * own
            pairs = pairs + lax.dot_general(
                spread, ahead, (((1,), (1,)), ((), ())), preferred_element_type=F32
            )
        return acc_k + acc_v, pairs

    def tap_rows(j, i):
        return pl.ds(pl.multiple_of((j * 24 + i // TAPS * 8 + i % TAPS) * 8, 8), 8)

    def tile_rows(j):
        return pl.ds(pl.multiple_of(j * STACK, STACK), STACK)

    @pl.loop(0, cols)
    def _(j):
        acc = forward(j, half)
        more, pairs = backward(j, 0)
        for i, value in enumerate(acc + more):
            tap_sums[tap_rows(j, i), :] = value
        for s in range(3):
            tap_sums[pl.ds(pl.multiple_of((j * 24 + s * 8 + TAPS) * 8, 8), 8), :] = jnp.zeros((8, LANES), F32)
        tabs[0, tile_rows(j), :] = pairs[:, :LANES]
        tabs[1, tile_rows(j), :BLOCK] = pairs[:, LANES:]

    pl.semaphore_wait(hear.at[0], len(x_peers + z_two))
    for peer in z_four:
        pl.semaphore_signal(hear.at[1], inc=1, device_id=peer, device_id_type=MESH)

    @pl.loop(0, cols)
    def _(j):
        prod_copy(j).wait_recv()
        mid_copy(j).wait_recv()

        @pl.when(first)
        def _():
            prod[j, pl.ds(0, LAGS), :] = jnp.zeros((LAGS, LANES), BF16)

        @pl.when(last)
        def _():
            mid[j, pl.ds(rows + HALO, LAGS - HALO), :] = jnp.zeros((LAGS - HALO, LANES), BF16)

        acc = forward(j, 0)
        more, pairs = backward(j, half)
        for i, value in enumerate(acc + more):
            tap_sums[tap_rows(j, i), :] += value
        tabs[0, tile_rows(j), :] += pairs[:, :LANES]
        tabs[1, tile_rows(j), :BLOCK] += pairs[:, LANES:]

    taps_total = tap_sums[pl.ds(0, cols * 24, stride=8), :]
    for b in range(1, 8):
        taps_total = taps_total + tap_sums[pl.ds(b, cols * 24, stride=8), :]
    lane = lax.broadcasted_iota(jnp.int32, (groups, LANES), 1)
    lags = tabs[0, pl.ds(0, groups, stride=BLOCK), :]
    for b in range(1, BLOCK):
        low = tabs[0, pl.ds(b, groups, stride=BLOCK), :]
        high = tabs[1, pl.ds(b, groups, stride=BLOCK), :]
        lags = lags + pltpu.roll(jnp.where(lane >= b, low, high), LANES - b, 1)
    for j in range(cols):
        pay[2 * j] = taps_total[j * 24 : j * 24 + 16]
        pay[2 * j + 1] = jnp.concatenate(
            [taps_total[j * 24 + 16 : j * 24 + 24], lags[j * per_col : (j + 1) * per_col]], axis=0
        )

    scatter = [
        remote(pay.at[index], got.at[i], s_rs.at[i], r_rs.at[i], device)
        for i, (index, device) in enumerate(team)
    ]
    for copy in scatter:
        copy.start()

    send_del = remote(
        delta.at[:, :, pl.ds(0, 8), :], delta.at[:, :, pl.ds(rows, 8), :], s_del.at[0], r_del.at[0], before
    )
    send_del.start()

    def adjoint(s, out_ref, spans):
        @pl.loop(0, cols)
        def _(j):
            taps = weights(s, j)
            for start, count in spans:
                total = taps[0] * delta[s, j, pl.ds(start, count), :]
                for tap in range(1, TAPS):
                    total = total + taps[tap] * delta[s, j, pl.ds(start + tap, count), :]
                out_ref[pl.ds(start, count), lanes_of(j)] = total.astype(BF16)

    body_spans = [(0, CHUNK), (CHUNK, CHUNK), (2 * CHUNK, CHUNK), (3 * CHUNK, CHUNK - HALO)]
    adjoint(0, gq_ref, body_spans)
    adjoint(1, gk_ref, body_spans)
    adjoint(2, gv_ref, body_spans)

    for copy in scatter:
        copy.wait_recv()
    mine = added([pay[me]] + [got[i] for i in range(len(team))])
    ring[z_far] = mine
    spread_far = [
        remote(ring.at[z_far], ring.at[z_far], s_far.at[i], r_far.at[i], device)
        for i, device in enumerate(far)
    ]
    pl.semaphore_wait(hear.at[1], len(z_four))
    for copy in spread_far:
        copy.start()

    send_del.wait_recv()

    @pl.when(last)
    def _():
        delta[:, :, pl.ds(rows, 8), :] = jnp.zeros((3, cols, 8, LANES), F32)

    for s, out_ref in enumerate((gq_ref, gk_ref, gv_ref)):
        adjoint(s, out_ref, [(rows - HALO, HALO)])
    stores = [
        pltpu.make_async_copy(src, dst, s_out.at[i])
        for i, (src, dst) in enumerate(((gq_ref, gq_hbm), (gk_ref, gk_hbm), (gv_ref, gv_hbm)))
    ]
    for copy in stores:
        copy.start()

    for i, device in enumerate(far):
        src = lax.rem(z_far + FAR - 1 - i, FAR)
        remote(ring.at[src], ring.at[src], s_far.at[i], r_far.at[i], device).wait_recv()
    mine = added([ring[i] for i in range(FAR)])
    full[me] = mine

    def squares(index):
        value = full[index].astype(F32)
        total = jnp.sum(jnp.sum(value * value, axis=0, keepdims=True), axis=1, keepdims=True)
        return jnp.broadcast_to(total, (1, LANES))

    seat = tp * TEAM + me
    own_norm[...] = squares(me)
    tell = [
        remote(own_norm, norms.at[seat], s_norm.at[i], r_norm.at[i], device)
        for i, (device, _) in enumerate(wide_team)
    ]
    gather = [
        remote(full.at[me], full.at[me], s_ag.at[i], r_ag.at[i], device) for i, (_, device) in enumerate(team)
    ]
    for copy in tell + gather:
        copy.start()
    for i, (_, device) in enumerate(team):
        remote(full.at[senders[i]], full.at[senders[i]], s_ag.at[i], r_ag.at[i], device).wait_recv()
    for index in range(TEAM):
        norms[tp * TEAM + index] = squares(index)
    for i, (device, src) in enumerate(wide_team):
        remote(norms.at[src], norms.at[src], s_norm.at[i], r_norm.at[i], device).wait_recv()
    total = added([norms[i] for i in range(NX * TEAM)])
    scale = 1.0 / jnp.maximum(1.0, jnp.sqrt(total) / CLIP)
    for j in range(cols):
        for s in range(3):
            part = full[2 * j + s // 2].astype(F32)[(s % 2) * 8 : (s % 2) * 8 + TAPS]
            gfeat_ref[s, :, pl.ds(j * LANES, LANES)] = scale * part
        gfilt_ref[pl.ds(j * per_col, per_col), :] = scale * full[2 * j + 1].astype(F32)[8:]

    @pl.loop(0, cols)
    def _(j):
        prod_copy(j).wait_send()
        mid_copy(j).wait_send()

    for copy in tails + aheads + [send_del] + scatter + spread_far + gather + tell:
        copy.wait_send()
    for copy in stores:
        copy.wait()


def emit(*refs):
    count = 5
    sources, targets, held = refs[:count], refs[count : 2 * count], refs[2 * count : 3 * count]
    s_in, s_out = refs[3 * count :]
    loads = [pltpu.make_async_copy(sources[i], held[i], s_in.at[i]) for i in range(count)]
    stores = [pltpu.make_async_copy(held[i], targets[i], s_out.at[i]) for i in range(count)]
    for copy in loads:
        copy.start()
    for load, store in zip(loads, stores):
        load.wait()
        store.start()
    for copy in stores:
        copy.wait()


def local(query_raw, key_raw, value_raw, cotangent, featurizer, filters):
    _, rows, channels = query_raw.shape
    groups = filters.shape[0]
    cols = channels // LANES
    flat = lambda x: x.reshape(rows, channels)
    vmem = pl.BlockSpec(memory_space=pltpu.VMEM)
    hbm = pl.BlockSpec(memory_space=pltpu.HBM)
    grad = jax.ShapeDtypeStruct((rows, channels), BF16)
    dma = pltpu.SemaphoreType.DMA
    shapes = (
        grad,
        grad,
        grad,
        jax.ShapeDtypeStruct(featurizer.shape, F32),
        jax.ShapeDtypeStruct(filters.shape, F32),
    )
    outs = pl.pallas_call(
        kernel,
        out_shape=shapes,
        in_specs=[hbm] * 6,
        out_specs=(hbm,) * 3 + (vmem,) * 2,
        scratch_shapes=[
            pltpu.VMEM((rows, channels), BF16),
            pltpu.VMEM((rows, channels), BF16),
            pltpu.VMEM((rows, channels), BF16),
            pltpu.VMEM((rows, channels), BF16),
            pltpu.VMEM((rows, channels), BF16),
            pltpu.VMEM((rows, channels), BF16),
            pltpu.VMEM((rows, channels), BF16),
            pltpu.VMEM(featurizer.shape, F32),
            pltpu.VMEM(filters.shape, BF16),
            pltpu.VMEM((3, HALO, channels), BF16),
            pltpu.VMEM((2, HALO, channels), BF16),
            pltpu.VMEM((3, cols, HALO + rows + HALO, LANES), F32),
            pltpu.VMEM((cols, rows, LANES), F32),
            pltpu.VMEM((cols, rows, LANES), F32),
            pltpu.VMEM((cols, LAGS + rows, LANES), BF16),
            pltpu.VMEM((cols, LAGS + rows, LANES), BF16),
            pltpu.VMEM((3, cols, rows + 8, LANES), F32),
            pltpu.VMEM((2, groups * BLOCK, LANES), F32),
            pltpu.VMEM((cols, STACK, 2 * LANES), BF16),
            pltpu.VMEM((cols, STACK, 2 * LANES), BF16),
            pltpu.VMEM((cols * 24 * 8, LANES), F32),
            pltpu.VMEM((TEAM, 16, LANES), F32),
            pltpu.VMEM((TEAM - 1, 16, LANES), F32),
            pltpu.VMEM((FAR, 16, LANES), F32),
            pltpu.VMEM((TEAM, 16, LANES), F32),
            pltpu.VMEM((NX * TEAM, 1, LANES), F32),
            pltpu.VMEM((1, LANES), F32),
            dma((6,)),
            dma((3,)),
            dma((3,)),
            dma((2,)),
            dma((2,)),
            dma((cols,)),
            dma((cols,)),
            dma((cols,)),
            dma((cols,)),
            dma((1,)),
            dma((1,)),
            dma((TEAM - 1,)),
            dma((TEAM - 1,)),
            dma((FAR - 1,)),
            dma((FAR - 1,)),
            dma((TEAM - 1,)),
            dma((TEAM - 1,)),
            dma(((NX - 1) * TEAM,)),
            dma(((NX - 1) * TEAM,)),
            dma((3,)),
            pltpu.SemaphoreType.REGULAR((2,)),
        ],
        compiler_params=pltpu.CompilerParams(
            collective_id=0, has_side_effects=True, vmem_limit_bytes=60 * 1024 * 1024
        ),
        cost_estimate=pl.CostEstimate(
            flops=12 * 256 * rows * channels, bytes_accessed=14 * rows * channels, transcendentals=0
        ),
    )(flat(query_raw), flat(key_raw), flat(value_raw), flat(cotangent), featurizer, filters)
    outs = pl.pallas_call(
        emit,
        out_shape=shapes,
        in_specs=[hbm] * 5,
        out_specs=(hbm,) * 5,
        scratch_shapes=[pltpu.VMEM(shape.shape, shape.dtype) for shape in shapes] + [dma((5,)), dma((5,))],
        compiler_params=pltpu.CompilerParams(vmem_limit_bytes=60 * 1024 * 1024),
    )(*outs)
    shape = query_raw.shape
    return (outs[0].reshape(shape), outs[1].reshape(shape), outs[2].reshape(shape), outs[3], outs[4])


def solution(mesh):
    stream = P(None, "ctx", "tp")
    return jax.shard_map(
        local,
        mesh=mesh,
        in_specs=(stream, stream, stream, stream, P(None, None, "tp"), P("tp", None)),
        out_specs=(stream, stream, stream, P(None, None, "tp"), P("tp", None)),
        check_vma=False,
    )
```
